512 devices in a mesh: dp: 32 (over z, y_hi), mp: 16 (over y_lo, x, core).
Axes of the slice: x: 4, y: 8 (y_hi: 4, y_lo: 2; y = y_hi * 2 + y_lo), z: 8, core: 2. Of those that a mesh axis runs over, the one named last changes fastest.
Arguments:
- inputs: bfloat16 [384, 256, 4096], P('dp', None, 'mp'), may hold values from -6 to 6
- cotangents: bfloat16 [384, 256, 4096], P('dp', None, 'mp'), may hold values from -6 to 6
- lengths: int32 [384], P('dp'), may hold values from 32 to 256
- reducing_matrix: bfloat16 [128, 4096], P(None, 'mp'), may hold values from -0.09375 to 0.09375
- expanding_matrix: bfloat16 [4096, 128], P('mp'), may hold values from -0.09375 to 0.09375
- width_sign_seeds: int32 [2, 256], replicated, may hold values from 0 to 1073741823
- rank_sign_seeds: int32 [2, 32], replicated, may hold values from 0 to 1073741823
- validation_projected: bfloat16 [2048, 8192], P('dp', 'mp'), may hold values from -6 to 6
Outputs:
- train_proj: float32 [384, 8192], P('dp', 'mp')
- influence: float32 [384, 8], replicated
The draws below stay inside these ranges and needn't reach their ends.
All inputs are finite; a program needn't handle non-finite values.
Results may differ from the reference program's by a relative error of at most 0.0003.
Values sent between devices are 32-bit elements; how exact they have to be, the bound alone decides.
A program may use at most 64 MiB of HBM per device.

```python
import math
import jax
import jax.numpy as jnp
from jax import lax

HIDDEN_SIZE = 4096
LOWRANK_DIM = 128
K1 = 32
K2 = 256
K = 8192
SEQUENCE_LEN = 256
TASKS = 8
E_ALL = 384
VAL = 2048


def with_ends(drawn, stream_key, least, top_value):
    index_at = [jax.random.randint(jax.random.fold_in(stream_key, axis), (), 0, length) for axis, length in enumerate(drawn.shape)]
    widest = drawn.shape.index(max(drawn.shape))
    neighbour = index_at[:widest] + [(index_at[widest] + 1) % drawn.shape[widest]] + index_at[widest + 1:]
    return drawn.at[tuple(index_at)].set(least).at[tuple(neighbour)].set(top_value)


def level_of(key, shape, split, least, high):
    loudness = 1.0
    for position, parts in split:
        heights = jax.random.uniform(jax.random.fold_in(jax.random.fold_in(key, 6), position), (parts,), jnp.float32, least / len(split), high / len(split))
        loudness = loudness * jnp.repeat(jnp.exp(heights), shape[position] // parts).reshape((-1,) + (1,) * (len(shape) - 1 - position))
    return loudness


def bell_draw(own_key, dims, spread, limit, split=(), kind=jnp.bfloat16):
    factor_of = level_of(own_key, dims, split, -0.22, 0.18) if split else 1.0
    array = jax.random.normal(own_key, dims, jnp.float32) * spread * factor_of
    return jnp.minimum(jnp.maximum(array, -limit), limit).astype(kind)


def setup_inputs(seed: int = 0) -> dict:
    arg_keys = jax.random.split(jax.random.key(seed), 9)
    inputs = bell_draw(arg_keys[0], (E_ALL, SEQUENCE_LEN, HIDDEN_SIZE), 1.0, 6.0, ((0, 32), (2, 16)))
    cotangents = bell_draw(arg_keys[1], (E_ALL, SEQUENCE_LEN, HIDDEN_SIZE), 1.0, 6.0, ((0, 32), (2, 16)))
    lengths = with_ends(jax.random.randint(arg_keys[2], (E_ALL,), SEQUENCE_LEN // 8, SEQUENCE_LEN + 1), jax.random.fold_in(arg_keys[2], 1), SEQUENCE_LEN // 8, SEQUENCE_LEN).astype(jnp.int32)
    reducing_matrix = bell_draw(arg_keys[3], (LOWRANK_DIM, HIDDEN_SIZE), HIDDEN_SIZE ** -0.5, 0.09375, ((1, 16),))
    expanding_matrix = bell_draw(arg_keys[4], (HIDDEN_SIZE, LOWRANK_DIM), HIDDEN_SIZE ** -0.5, 0.09375, ((0, 16),))
    width_sign_seeds = with_ends(jax.random.randint(arg_keys[5], (2, K2), 0, 1073741824), jax.random.fold_in(arg_keys[5], 1), 0, 1073741823).astype(jnp.int32)
    rank_sign_seeds = with_ends(jax.random.randint(arg_keys[6], (2, K1), 0, 1073741824), jax.random.fold_in(arg_keys[6], 1), 0, 1073741823).astype(jnp.int32)
    validation_projected = bell_draw(arg_keys[7], (VAL, K), 1.0, 6.0, ((0, 32), (1, 16)))
    return dict(inputs=inputs, cotangents=cotangents, lengths=lengths, reducing_matrix=reducing_matrix, expanding_matrix=expanding_matrix, width_sign_seeds=width_sign_seeds, rank_sign_seeds=rank_sign_seeds, validation_projected=validation_projected)


epsilon = 1e-06

def sign_table(seed_rows, column_ids):
    mixed = seed_rows[:, None] + column_ids[None, :] * 747796405
    for multiplier, distance in ((1103515245, 16), (1664525, 13), (22695477, 16)):
        mixed = mixed & 2147483647
        mixed = mixed ^ jnp.right_shift(mixed, distance)
        mixed = mixed * multiplier
    mixed = mixed & 2147483647
    parity = jnp.right_shift(mixed, 17) & 1
    return (1 - 2 * parity).astype(jnp.float32)

def reference(inputs, cotangents, lengths, reducing_matrix, expanding_matrix, width_sign_seeds, rank_sign_seeds, validation_projected):
    top_score = lax.Precision.HIGHEST
    column_ids = jnp.arange(HIDDEN_SIZE, dtype=jnp.int32)
    right_a = sign_table(width_sign_seeds[0], column_ids).astype(jnp.bfloat16).astype(jnp.float32)
    right_b = sign_table(width_sign_seeds[1], column_ids).astype(jnp.bfloat16).astype(jnp.float32)
    lowrank_coordinate = jnp.arange(LOWRANK_DIM, dtype=jnp.int32)
    left_a = sign_table(rank_sign_seeds[0], lowrank_coordinate)
    left_b = sign_table(rank_sign_seeds[1], lowrank_coordinate)
    expanding_wide = expanding_matrix.astype(jnp.float32)
    reducing_wide = reducing_matrix.astype(jnp.float32)
    positions = jnp.arange(SEQUENCE_LEN, dtype=jnp.int32)
    sketch_multiplier = 1.0 / math.sqrt(2.0 * LOWRANK_DIM * HIDDEN_SIZE * SEQUENCE_LEN)

    def one_example(example_item):
        tokens, cotangent, length = example_item
        token_keep = (positions < length).astype(jnp.bfloat16)[:, None]
        input_masked = (tokens * token_keep).astype(jnp.float32)
        result_zeroed_pad = (cotangent * token_keep).astype(jnp.float32)
        adapter_output = jnp.dot(result_zeroed_pad, expanding_wide, precision=top_score)
        adapter_input = jnp.dot(input_masked, reducing_wide.T, precision=top_score)
        projected_input = jnp.dot(input_masked, right_a.T, precision=top_score)
        projected_output = jnp.dot(result_zeroed_pad, right_b.T, precision=top_score)
        down_inner = jnp.dot(adapter_output.T, projected_input, precision=top_score)
        up_inner = jnp.dot(adapter_input.T, projected_output, precision=top_score)
        combined = jnp.dot(left_a, down_inner, precision=top_score) + jnp.dot(left_b, up_inner, precision=top_score)
        return (combined * sketch_multiplier).reshape(K1 * K2)
    train_proj = lax.map(one_example, (inputs, cotangents, lengths))
    train_sq = lax.optimization_barrier(jnp.sum(train_proj * train_proj, axis=1))
    unit_train = train_proj * lax.rsqrt(train_sq + epsilon)[:, None]
    val_wide = validation_projected.astype(jnp.float32)
    val_sq = lax.optimization_barrier(jnp.sum(val_wide * val_wide, axis=1))
    unit_val = val_wide * lax.rsqrt(val_sq + epsilon)[:, None]
    scores = jnp.dot(unit_train, unit_val.T, precision=top_score) * math.sqrt(K)
    grouped = scores.reshape(E_ALL, TASKS, VAL // TASKS)
    influence = lax.optimization_barrier(jnp.max(grouped, axis=2))
    return (train_proj, influence)
```

```python
import functools
import math

import jax
import jax.numpy as jnp
from jax import lax
from jax.experimental import pallas as pl
from jax.experimental.pallas import tpu as pltpu
from jax.sharding import PartitionSpec as P

MESH = pl.DeviceIdType.MESH
EPSILON = 1e-06
LOWEST = -3e38
F32 = jnp.float32
BF16 = jnp.bfloat16

NT = (((1,), (1,)), ((), ()))
NN = (((1,), (0,)), ((), ()))


def sign_of(seeds, columns):
    mixed = seeds + columns * 747796405
    for multiplier, distance in ((1103515245, 16), (1664525, 13), (22695477, 16)):
        mixed = mixed & 2147483647
        mixed = mixed ^ jnp.right_shift(mixed, distance)
        mixed = mixed * multiplier
    mixed = mixed & 2147483647
    parity = jnp.right_shift(mixed, 17) & 1
    return (1 - 2 * parity).astype(F32)


def dot(a, b, dims):
    return lax.dot_general(a, b, dims, preferred_element_type=F32)


def split(value):
    high = value.astype(BF16)
    return high, (value - high.astype(F32)).astype(BF16)


def kernel(
    nz,
    nyh,
    nq,
    scale,
    root_k,
    x_ref,
    g_ref,
    len_ref,
    red_ref,
    exp_ref,
    wseed_ref,
    rseed_ref,
    val_ref,
    tp_ref,
    inf_ref,
    x_v,
    g_v,
    red_v,
    exp_v,
    wseed_v,
    rseed_v,
    rpad,
    val_v,
    u,
    r1,
    r2,
    uf,
    ra,
    rb,
    ha,
    hb,
    t,
    ts,
    r3,
    r4,
    tg,
    lt,
    vf,
    vb,
    sc,
    r5,
    fy,
    fz,
    in_sem,
    small_sem,
    s1,
    d1,
    s2,
    d2,
    s3,
    d3,
    s4,
    d4,
    s5,
    d5,
    s6,
    d6,
    s7,
    d7,
    sv,
    dv,
    s8,
    d8,
    s9,
    d9,
    s10,
    d10,
    s11,
    d11,
):
    nmp = 2 * nq
    el = x_v.shape[0]
    k1 = nmp * 2
    per = 2 * k1
    half_e = el // 2
    half_rows = half_e * per
    chunk = half_rows // nq
    tokens = x_v.shape[1]
    width = x_v.shape[2]
    vl = val_v.shape[0]
    te = 2 * el
    er = nyh * el // nmp
    hv = nz * vl // 2

    dp = lax.axis_index("dp")
    m = lax.axis_index("mp")
    q = lax.div(m, 2)
    c = lax.rem(m, 2)
    other = 1 - c
    z = lax.div(dp, nyh)
    yh = lax.rem(dp, nyh)
    sibling = (dp, 2 * q + other)

    def chip(p):
        return (dp, 2 * p + c)

    def plane(zz):
        return (zz * nyh + yh, m)

    def row(yy):
        return (z * nyh + yy, m)

    def remote(src, dst, send, recv, device):
        return pltpu.make_async_remote_copy(
            src_ref=src, dst_ref=dst, send_sem=send, recv_sem=recv, device_id=device, device_id_type=MESH
        )

    def input_copies(e):
        return (
            pltpu.make_async_copy(x_ref.at[e], x_v.at[e], in_sem.at[0, e]),
            pltpu.make_async_copy(g_ref.at[e], g_v.at[e], in_sem.at[1, e]),
        )

    small = [
        pltpu.make_async_copy(a, b, small_sem.at[i])
        for i, (a, b) in enumerate(
            (
                (rseed_ref, rseed_v),
                (red_ref, red_v),
                (exp_ref, exp_v),
                (val_ref, val_v),
                (wseed_ref, wseed_v),
            )
        )
    ]
    for copy in small:
        copy.start()

    def order(i):
        return lax.rem(other * half_e + i, el)

    def start_inputs(i, carry):
        for copy in input_copies(order(i)):
            copy.start()
        return carry

    lax.fori_loop(0, el, start_inputs, 0)

    barrier = pltpu.get_barrier_semaphore()

    def greet(device):
        pl.semaphore_signal(barrier, inc=1, device_id=device, device_id_type=MESH)

    def greet_mp(j, carry):
        greet((dp, lax.rem(m + j, nmp)))
        return carry

    lax.fori_loop(1, nmp, greet_mp, 0)
    for j in range(1, nz):
        greet(plane(lax.rem(z + j, nz)))
    for j in range(1, nyh):
        greet(row(lax.rem(yh + j, nyh)))

    small[0].wait()
    rpad[...] = jnp.zeros_like(rpad)
    rpad[0:2, 0:k1] = rseed_v[...]
    ranks = lax.broadcasted_iota(jnp.int32, (128, 128), 0)
    left_a = sign_of(rpad[0:1, :], ranks).T[0:k1].astype(BF16)
    left_b = sign_of(rpad[1:2, :], ranks).T[0:k1].astype(BF16)
    small[1].wait()
    small[2].wait()
    p_out = jnp.concatenate(split(dot(left_a, exp_v[...], NT)), axis=0)
    p_in = jnp.concatenate(split(dot(left_b, red_v[...], NN)), axis=0)

    lane_t = lax.broadcasted_iota(jnp.int32, (k1, tokens), 1)

    def sketch(i, carry):
        e = order(i)
        for copy in input_copies(e):
            copy.wait()
        kept = lane_t < len_ref[e]
        out = dot(p_out, g_v[e], NT)
        inn = dot(p_in, x_v[e], NT)
        base = pl.multiple_of(e * per, per)
        u[pl.ds(base, k1), :] = jnp.where(kept, out[:k1] + out[k1:], 0.0)
        u[pl.ds(base + k1, k1), :] = jnp.where(kept, inn[:k1] + inn[k1:], 0.0)
        return carry

    def u_half(h):
        return u.at[pl.ds(pl.multiple_of(h * half_rows, half_rows), half_rows)]

    def rows_of(h, p):
        return pl.ds(pl.multiple_of(h * half_rows + p * chunk, chunk), chunk)

    lax.fori_loop(0, half_e, sketch, 0)

    pl.semaphore_wait(barrier, (nmp - 1) + (nz - 1) + (nyh - 1))

    to_sibling = remote(u_half(other), r1, s1.at[0], d1.at[0], sibling)
    to_sibling.start()

    small[3].wait()
    vf[z] = val_v[...].astype(F32)
    steps = nz // 2
    up = plane(lax.rem(z + 1, nz))
    down = plane(lax.rem(z + nz - 1, nz))

    def ring(step):
        a = lax.rem(z + nz - step, nz)
        b = lax.rem(z + step, nz)
        if step < steps - 1:
            first, second = vf.at[a], vf.at[b]
        else:
            first, second = vf.at[a, pl.ds(0, vl // 2)], vf.at[b, pl.ds(vl // 2, vl // 2)]
        return (
            remote(first, first, sv.at[0, step], dv.at[0, step], up),
            remote(second, second, sv.at[1, step], dv.at[1, step], down),
        )

    def ring_start(step):
        for copy in ring(step):
            copy.start()

    def ring_wait(step):
        for copy in ring(step):
            copy.wait_recv()

    ring_start(0)

    lax.fori_loop(half_e, el, sketch, 0)

    to_sibling.wait_recv()

    def spread(j):
        p = lax.rem(q + j, nq)
        return remote(u.at[rows_of(c, p)], r2.at[j - 1], s2.at[j - 1], d2.at[j - 1], chip(p))

    for j in range(1, nq):
        p = lax.rem(q + j, nq)
        u[rows_of(c, p), :] += r1[pl.ds(pl.multiple_of(p * chunk, chunk), chunk), :]
        spread(j).start()
    ring_wait(0)
    if steps > 1:
        ring_start(1)

    small[4].wait()
    columns = m * width + lax.broadcasted_iota(jnp.int32, (width, wseed_v.shape[1]), 0)
    ra[...] = sign_of(wseed_v[0:1, :], columns).astype(BF16)
    rb[...] = sign_of(wseed_v[1:2, :], columns).astype(BF16)

    own = u[rows_of(c, q), :] + r1[pl.ds(pl.multiple_of(q * chunk, chunk), chunk), :]
    for j in range(1, nq):
        spread(j).wait_recv()
        own = own + r2[j - 1]
    uf[rows_of(c, q), :] = own

    def hand_out(j):
        part = uf.at[rows_of(c, q)]
        return remote(part, part, s3.at[j - 1], d3.at[j - 1], chip(lax.rem(q + j, nq)))

    def landed(j):
        part = uf.at[rows_of(c, lax.rem(q + nq - j, nq))]
        return remote(part, part, s3.at[j - 1], d3.at[j - 1], chip(lax.rem(q + nq - j, nq)))

    def pass_on(j):
        part = uf.at[rows_of(c, lax.rem(q + nq - j, nq))]
        return remote(part, part, s4.at[j], d4.at[j], sibling)

    def passed(j):
        part = uf.at[rows_of(other, lax.rem(q + nq - j, nq))]
        return remote(part, part, s4.at[j], d4.at[j], sibling)

    for j in range(1, nq):
        hand_out(j).start()
    pass_on(0).start()
    if steps > 1:
        ring_wait(1)
    if steps > 2:
        ring_start(2)
    for j in range(1, nq):
        landed(j).wait_recv()
        pass_on(j).start()

    def project(first):
        def body(i, carry):
            e = first + i
            base = pl.multiple_of(e * per, per)
            a = jnp.concatenate(split(uf[pl.ds(base, k1), :]), axis=0)
            b = jnp.concatenate(split(uf[pl.ds(base + k1, k1), :]), axis=0)
            down_part = dot(a, x_v[e], NN)
            up_part = dot(b, g_v[e], NN)
            at = pl.ds(pl.multiple_of(e * k1, k1), k1)
            high, low = split(down_part[:k1] + down_part[k1:])
            ha[0, at, :] = high
            ha[1, at, :] = low
            high, low = split(up_part[:k1] + up_part[k1:])
            hb[0, at, :] = high
            hb[1, at, :] = low
            return carry

        return body

    lax.fori_loop(0, half_e, project(c * half_e), 0)
    for j in range(nq):
        passed(j).wait_recv()
    if steps > 2:
        ring_wait(2)
    if steps > 3:
        ring_start(3)
    lax.fori_loop(0, half_e, project(other * half_e), 0)

    block = el * k1 // 3

    def combine(i, carry):
        at = pl.ds(pl.multiple_of(i * block, block), block)
        total = dot(ha[0, at, :], ra[...], NN) + dot(hb[0, at, :], rb[...], NN)
        total = total + (dot(ha[1, at, :], ra[...], NN) + dot(hb[1, at, :], rb[...], NN))
        total = total * scale
        t[0, at, :] = total[:, :128]
        t[1, at, :] = total[:, 128:]
        return carry

    lax.fori_loop(0, 3, combine, 0)
    for a in range(k1):
        cc, qq, al = (a // 2) % 2, a // 4, a % 2
        for side in range(2):
            ts[cc, qq, al * el : (al + 1) * el, side * 128 : (side + 1) * 128] = t[
                side, pl.ds(a, el, stride=k1), :
            ]

    swap = remote(ts.at[other], r3, s5.at[0], d5.at[0], sibling)
    swap.start()
    if steps > 3:
        ring_wait(3)

    swap.wait_recv()

    def scatter(j):
        p = lax.rem(q + j, nq)
        return remote(ts.at[c, p], r4.at[j - 1], s6.at[j - 1], d6.at[j - 1], chip(p))

    for j in range(1, nq):
        p = lax.rem(q + j, nq)
        ts[c, p] += r3[p]
        scatter(j).start()

    def narrow(i, carry):
        vb[pl.ds(pl.multiple_of(i * vl, vl), vl), :] = vf[i].astype(BF16)
        return carry

    lax.fori_loop(0, nz, narrow, 0)
    ones = jnp.ones((16, vf.shape[2]), BF16)
    sc[...] = jnp.zeros_like(sc)
    for side in range(2):
        wide = vb[side * hv : (side + 1) * hv, :].astype(F32)
        high, low = split(wide * wide)
        norms = dot(ones, high, NT) + dot(ones, low, NT)

        def place(i, carry, norms=norms, side=side):
            sc[i, 2 * er + side : 2 * er + side + 1, 0:hv] = norms[0:1]
            return carry

        lax.fori_loop(0, nmp, place, 0)

    total = ts[c, q] + r3[q]
    for j in range(1, nq):
        scatter(j).wait_recv()
        total = total + r4[j - 1]
    tg[yh] = total
    tp_ref[:, 0:256] = total[0:el]
    tp_ref[:, 256:512] = total[el:te]

    def share(j):
        part = tg.at[yh]
        return remote(part, part, s7.at[j - 1], d7.at[j - 1], row(lax.rem(yh + j, nyh)))

    def shared(j):
        part = tg.at[lax.rem(yh + nyh - j, nyh)]
        return remote(part, part, s7.at[j - 1], d7.at[j - 1], row(lax.rem(yh + nyh - j, nyh)))

    for j in range(1, nyh):
        share(j).start()
    for j in range(1, nyh):
        shared(j).wait_recv()

    for y in range(nyh):
        for al in range(2):
            lt[y * el : (y + 1) * el, al * 256 : (al + 1) * 256] = tg[y, al * el : (al + 1) * el, :]
    train = lt[...]
    rows = nyh * el
    high, low = split(train)
    scores = dot(high, vb[...], NT) + dot(low, vb[...], NT)
    squares = jnp.broadcast_to(jnp.sum(train * train, axis=1, keepdims=True), (rows, 128))
    for i in range(nmp):
        sc[i, 0:er, 0:hv] = scores[i * er : (i + 1) * er, 0:hv]
        sc[i, er : 2 * er, 0:hv] = scores[i * er : (i + 1) * er, hv : 2 * hv]
        sc[i, 0:er, hv : hv + 128] = squares[i * er : (i + 1) * er]
        sc[i, er : 2 * er, hv : hv + 128] = squares[i * er : (i + 1) * er]

    def deal(j):
        p = lax.rem(m + j, nmp)
        return remote(sc.at[p], r5.at[j - 1], s8.at[j - 1], d8.at[j - 1], (dp, p))

    def deal_start(j, carry):
        deal(j).start()
        return carry

    def deal_wait(j, carry):
        deal(j).wait_recv()
        return carry + r5[j - 1]

    lax.fori_loop(1, nmp, deal_start, 0)
    summed = lax.fori_loop(1, nmp, deal_wait, sc[m])

    row_id = lax.broadcasted_iota(jnp.int32, (8, hv), 0)
    lane_id = lax.broadcasted_iota(jnp.int32, (8, hv), 1)
    norms = jnp.where(row_id < er, summed[2 * er : 2 * er + 1, 0:hv], summed[2 * er + 1 : 2 * er + 2, 0:hv])
    cosines = summed[:, 0:hv] * lax.rsqrt(norms + EPSILON)
    weight = lax.rsqrt(summed[:, hv : hv + 1] + EPSILON) * root_k
    row_o = lax.broadcasted_iota(jnp.int32, (8, 128), 0)
    lane_o = lax.broadcasted_iota(jnp.int32, (8, 128), 1)
    placed = jnp.full((8, 128), LOWEST, F32)
    first_half = row_o < er
    e_of = jnp.where(first_half, row_o, row_o - er)
    for g in range(nz // 2):
        here = (lane_id >= g * vl) & (lane_id < (g + 1) * vl)
        best = jnp.max(jnp.where(here, cosines, LOWEST), axis=1, keepdims=True) * weight
        lane = e_of * nz + jnp.where(first_half, 0, nz // 2) + g
        placed = jnp.where((lane_o == lane) & (row_o < 2 * er), best, placed)
    fy[0] = jnp.max(placed, axis=0, keepdims=True)

    def merge(j):
        return remote(fy.at[0], fy.at[j], s9.at[j - 1], d9.at[j - 1], row(lax.rem(yh + j, nyh)))

    for j in range(1, nyh):
        merge(j).start()
    best = fy[0]
    for j in range(1, nyh):
        merge(j).wait_recv()
        best = jnp.maximum(best, fy[j])
    fz[z, m] = best

    def tell(j):
        part = fz.at[z, m]
        return remote(part, part, s10.at[j - 1], d10.at[j - 1], (dp, lax.rem(m + j, nmp)))

    def told(j):
        p = lax.rem(m + nmp - j, nmp)
        part = fz.at[z, p]
        return remote(part, part, s10.at[j - 1], d10.at[j - 1], (dp, p))

    def tell_start(j, carry):
        tell(j).start()
        return carry

    def told_wait(j, carry):
        told(j).wait_recv()
        return carry

    lax.fori_loop(1, nmp, tell_start, 0)
    lax.fori_loop(1, nmp, told_wait, 0)

    def publish(j):
        part = fz.at[z]
        return remote(part, part, s11.at[j - 1], d11.at[j - 1], plane(lax.rem(z + j, nz)))

    def published(j):
        zz = lax.rem(z + nz - j, nz)
        part = fz.at[zz]
        return remote(part, part, s11.at[j - 1], d11.at[j - 1], plane(zz))

    for j in range(1, nz):
        publish(j).start()
    for j in range(1, nz):
        published(j).wait_recv()
    inf_ref[...] = fz[...]

    to_sibling.wait_send()
    swap.wait_send()
    for j in range(1, nq):
        spread(j).wait_send()
        hand_out(j).wait_send()
        scatter(j).wait_send()
    for j in range(nq):
        pass_on(j).wait_send()
    for step in range(steps):
        for copy in ring(step):
            copy.wait_send()
    for j in range(1, nyh):
        share(j).wait_send()
        merge(j).wait_send()
    for j in range(1, nz):
        publish(j).wait_send()

    def last(j, carry):
        deal(j).wait_send()
        tell(j).wait_send()
        return carry

    lax.fori_loop(1, nmp, last, 0)


def on_device(nz, nyh, nq, scale, root_k, *args):
    inputs, _, _, reducing, expanding, wseeds, rseeds, validation = args
    el, tokens, width = inputs.shape
    nmp = 2 * nq
    k1 = 2 * nmp
    vl, kl = validation.shape
    k2 = wseeds.shape[1]
    half_rows = el * k1
    chunk = half_rows // nq
    hv = nz * vl // 2
    dma = pltpu.SemaphoreType.DMA
    anywhere = pl.BlockSpec(memory_space=pl.ANY)
    vmem = pl.BlockSpec(memory_space=pltpu.VMEM)
    scratch = [
        pltpu.VMEM(inputs.shape, BF16),
        pltpu.VMEM(inputs.shape, BF16),
        pltpu.VMEM(reducing.shape, BF16),
        pltpu.VMEM(expanding.shape, BF16),
        pltpu.VMEM(wseeds.shape, jnp.int32),
        pltpu.VMEM(rseeds.shape, jnp.int32),
        pltpu.VMEM((8, 128), jnp.int32),
        pltpu.VMEM(validation.shape, BF16),
        pltpu.VMEM((2 * half_rows, tokens), F32),
        pltpu.VMEM((half_rows, tokens), F32),
        pltpu.VMEM((nq - 1, chunk, tokens), F32),
        pltpu.VMEM((2 * half_rows, tokens), F32),
        pltpu.VMEM((width, k2), BF16),
        pltpu.VMEM((width, k2), BF16),
        pltpu.VMEM((2, el * k1, width), BF16),
        pltpu.VMEM((2, el * k1, width), BF16),
        pltpu.VMEM((2, el * k1, 128), F32),
        pltpu.VMEM((2, nq, 2 * el, k2), F32),
        pltpu.VMEM((nq, 2 * el, k2), F32),
        pltpu.VMEM((nq - 1, 2 * el, k2), F32),
        pltpu.VMEM((nyh, 2 * el, k2), F32),
        pltpu.VMEM((nyh * el, kl), F32),
        pltpu.VMEM((nz, vl, kl), F32),
        pltpu.VMEM((nz * vl, kl), BF16),
        pltpu.VMEM((nmp, 8, hv + 128), F32),
        pltpu.VMEM((nmp - 1, 8, hv + 128), F32),
        pltpu.VMEM((nyh, 1, 128), F32),
        pltpu.VMEM((nz, nmp, 1, 128), F32),
        dma((2, el)),
        dma((5,)),
    ]
    ring = (2, nz // 2)
    for count in (
        (1,),
        (nq - 1,),
        (nq - 1,),
        (nq,),
        (1,),
        (nq - 1,),
        (max(nyh - 1, 1),),
        ring,
        (nmp - 1,),
        (max(nyh - 1, 1),),
        (nmp - 1,),
        (nz - 1,),
    ):
        scratch += [dma(count), dma(count)]
    train_proj, best = pl.pallas_call(
        functools.partial(kernel, nz, nyh, nq, scale, root_k),
        out_shape=(
            jax.ShapeDtypeStruct((el, kl), F32),
            jax.ShapeDtypeStruct((nz, nmp, 1, 128), F32),
        ),
        in_specs=[
            anywhere,
            anywhere,
            pl.BlockSpec(memory_space=pltpu.SMEM),
            anywhere,
            anywhere,
            anywhere,
            anywhere,
            anywhere,
        ],
        out_specs=(vmem, vmem),
        scratch_shapes=scratch,
        compiler_params=pltpu.CompilerParams(
            collective_id=0, has_side_effects=True, vmem_limit_bytes=48 * 1024 * 1024
        ),
    )(*args)
    er = nyh * el // nmp
    influence = best.reshape(nz * nmp, 128)[:, : er * nz].reshape(nz * nmp * er, nz)
    return (train_proj, influence)


def solution(mesh, nyh=4):
    ndp, nmp = mesh.shape["dp"], mesh.shape["mp"]
    nz, nq = ndp // nyh, nmp // 2
    width = nmp * 256
    scale = 1.0 / math.sqrt(2.0 * 128 * width * 256)
    root_k = math.sqrt(2 * nmp * 256)
    in_specs = (
        P("dp", None, "mp"),
        P("dp", None, "mp"),
        P("dp"),
        P(None, "mp"),
        P("mp", None),
        P(),
        P(),
        P("dp", "mp"),
    )
    return jax.shard_map(
        functools.partial(on_device, nz, nyh, nq, scale, root_k),
        mesh=mesh,
        in_specs=in_specs,
        out_specs=(P("dp", "mp"), P()),
        check_vma=False,
    )
```

```python
import functools
import math

import jax
import jax.numpy as jnp
from jax import lax
from jax.experimental import pallas as pl
from jax.experimental.pallas import tpu as pltpu
from jax.sharding import PartitionSpec as P

MESH = pl.DeviceIdType.MESH
EPSILON = 1e-06
LOWEST = -3e38
F32 = jnp.float32
BF16 = jnp.bfloat16

NT = (((1,), (1,)), ((), ()))
NN = (((1,), (0,)), ((), ()))


def sign_of(seeds, columns):
    mixed = seeds + columns * 747796405
    for multiplier, distance in ((1103515245, 16), (1664525, 13), (22695477, 16)):
        mixed = mixed & 2147483647
        mixed = mixed ^ jnp.right_shift(mixed, distance)
        mixed = mixed * multiplier
    mixed = mixed & 2147483647
    parity = jnp.right_shift(mixed, 17) & 1
    return (1 - 2 * parity).astype(F32)


def dot(a, b, dims):
    return lax.dot_general(a, b, dims, preferred_element_type=F32)


def split(value):
    high = value.astype(BF16)
    return high, (value - high.astype(F32)).astype(BF16)


def kernel(nz, nyh, nq, np_, scale, root_k, *refs):
    (
        (x_ref, g_ref, len_ref, red_ref, exp_ref, wseed_ref, rseed_ref, val_ref, tp_ref, inf_ref),
        (x_v, g_v, len_v, red_v, exp_v, wseed_v, rseed_v, rpad, val_v, u, r1, r2, uf, ra, rb, ha, hb, t, ts, r3, r4),
        (tg, lt, vf, vb, vq, rq, sc, r5, fp, fz),
        (in_sem, small_sem, s1, d1, s2, d2, s3, d3, s4, d4, s5, d5, s6, d6, s7, d7, sv, dv, sq, dq, s8, d8, s9, d9, s10, d10),
    ) = refs[:10], refs[10:31], refs[31:41], refs[41:]
    nmp = 2 * nq
    el = x_v.shape[0]
    k1 = nmp * 2
    per = 2 * k1
    half_e = el // 2
    piece_e = half_e // np_
    half_rows = half_e * per
    piece_rows = piece_e * per
    chunk = piece_rows // nq
    tokens = x_v.shape[1]
    width = x_v.shape[2]
    vl = val_v.shape[0]
    te = 2 * el
    er = nyh * el // nmp
    hv = nz * vl // 2

    dp = lax.axis_index("dp")
    m = lax.axis_index("mp")
    q = lax.div(m, 2)
    c = lax.rem(m, 2)
    other = 1 - c
    z = lax.div(dp, nyh)
    yh = lax.rem(dp, nyh)
    sibling = (dp, 2 * q + other)

    def chip(p):
        return (dp, 2 * p + c)

    def column(zz):
        return (zz * nyh + yh, m)

    def row(yy, mm):
        return (z * nyh + yy, mm)

    def remote(src, dst, send, recv, device):
        return pltpu.make_async_remote_copy(
            src_ref=src, dst_ref=dst, send_sem=send, recv_sem=recv, device_id=device, device_id_type=MESH
        )

    pieces = [(h, k) for h in (other, c) for k in range(np_)]

    def examples(h, k):
        return pl.ds(h * half_e + k * piece_e, piece_e)

    inputs = []
    for i, (h, k) in enumerate(pieces):
        inputs.append(
            (
                pltpu.make_async_copy(x_ref.at[examples(h, k)], x_v.at[examples(h, k)], in_sem.at[0, i]),
                pltpu.make_async_copy(g_ref.at[examples(h, k)], g_v.at[examples(h, k)], in_sem.at[1, i]),
            )
        )
    small = [
        pltpu.make_async_copy(a, b, small_sem.at[i])
        for i, (a, b) in enumerate(
            (
                (rseed_ref, rseed_v),
                (red_ref, red_v),
                (exp_ref, exp_v),
                (len_ref, len_v),
                (val_ref, val_v),
                (wseed_ref, wseed_v),
            )
        )
    ]
    for copy in small[:4]:
        copy.start()
    for pair in inputs:
        for copy in pair:
            copy.start()
    for copy in small[4:]:
        copy.start()

    barrier = pltpu.get_barrier_semaphore()

    def greet(device):
        pl.semaphore_signal(barrier, inc=1, device_id=device, device_id_type=MESH)

    others = [(dy, dm) for dy in range(nyh) for dm in range(nmp) if (dy, dm) != (0, 0)]

    def neighbour(dy, dm):
        return lax.rem(yh + dy, nyh), lax.rem(m + dm, nmp)

    for dy, dm in others:
        greet(row(*neighbour(dy, dm)))
    for j in range(1, nz):
        greet(column(lax.rem(z + j, nz)))

    rpad[...] = jnp.zeros_like(rpad)
    small[0].wait()
    rpad[0:2, 0:k1] = rseed_v[...]
    ranks = lax.broadcasted_iota(jnp.int32, (128, 128), 0)
    left_a = sign_of(rpad[0:1, :], ranks).T[0:k1].astype(BF16)
    left_b = sign_of(rpad[1:2, :], ranks).T[0:k1].astype(BF16)
    small[1].wait()
    small[2].wait()
    p_out = jnp.concatenate(split(dot(left_a, exp_v[...], NT)), axis=0)
    p_in = jnp.concatenate(split(dot(left_b, red_v[...], NN)), axis=0)
    small[3].wait()

    lane_t = lax.broadcasted_iota(jnp.int32, (k1, tokens), 1)

    def sketch(first):
        def body(i, carry):
            e = first + i
            kept = lane_t < len_v[e]
            out = dot(p_out, g_v[e], NT)
            inn = dot(p_in, x_v[e], NT)
            base = pl.multiple_of(e * per, per)
            u[pl.ds(base, k1), :] = jnp.where(kept, out[:k1] + out[k1:], 0.0)
            u[pl.ds(base + k1, k1), :] = jnp.where(kept, inn[:k1] + inn[k1:], 0.0)
            return carry

        return body

    def sketch_piece(i):
        h, k = pieces[i]
        for copy in inputs[i]:
            copy.wait()
        lax.fori_loop(0, piece_e, sketch(h * half_e + k * piece_e), 0)

    def rows_of(h, k):
        return pl.ds(pl.multiple_of(h * half_rows + k * piece_rows, piece_rows), piece_rows)

    def chunk_of(h, k, p):
        return pl.ds(pl.multiple_of(h * half_rows + k * piece_rows + p * chunk, chunk), chunk)

    def lend(k):
        return remote(u.at[rows_of(other, k)], r1.at[k], s1.at[k], d1.at[k], sibling)

    def spread(k, j):
        p = lax.rem(q + j, nq)
        return remote(u.at[chunk_of(c, k, p)], r2.at[k, j - 1], s2.at[k], d2.at[k], chip(p))

    def spread_all(k):
        return remote(r2.at[k], r2.at[k], s2.at[k], d2.at[k], chip(q))

    def borrowed(k, p):
        return u[chunk_of(c, k, p), :] + r1[k, pl.ds(pl.multiple_of(p * chunk, chunk), chunk), :]

    def spread_piece(k):
        lend(k).wait_recv()
        for j in range(1, nq):
            p = lax.rem(q + j, nq)
            u[chunk_of(c, k, p), :] = borrowed(k, p)
            spread(k, j).start()

    steps = nz // 2
    up = column(lax.rem(z + 1, nz))
    down = column(lax.rem(z + nz - 1, nz))

    def ring(step):
        a = lax.rem(z + nz - step, nz)
        b = lax.rem(z + step, nz)
        if step < steps - 1:
            first, second = vf.at[a], vf.at[b]
        else:
            first, second = vf.at[a, pl.ds(0, vl // 2)], vf.at[b, pl.ds(vl // 2, vl // 2)]
        return (
            remote(first, first, sv.at[0, step], dv.at[0, step], up),
            remote(second, second, sv.at[1, step], dv.at[1, step], down),
        )

    def ring_start(step):
        if step < steps:
            for copy in ring(step):
                copy.start()

    def ring_wait(step):
        if step < steps:
            for copy in ring(step):
                copy.wait_recv()

    sketch_piece(0)
    pl.semaphore_wait(barrier, len(others) + nz - 1)
    lend(0).start()
    for k in range(1, np_):
        sketch_piece(k)
        lend(k).start()
    for k in range(np_):
        sketch_piece(np_ + k)
        spread_piece(k)
        if k == 0:
            small[4].wait()
            vf[z] = val_v[...].astype(F32)
            ring_start(0)

    small[5].wait()
    columns = m * width + lax.broadcasted_iota(jnp.int32, (width, wseed_v.shape[1]), 0)
    ra[...] = sign_of(wseed_v[0:1, :], columns).astype(BF16)
    rb[...] = sign_of(wseed_v[1:2, :], columns).astype(BF16)

    def hand_out(k, j):
        part = uf.at[chunk_of(c, k, q)]
        return remote(part, part, s3.at[k, j - 1], d3.at[k, j - 1], chip(lax.rem(q + j, nq)))

    def landed(k, j):
        p = lax.rem(q + nq - j, nq)
        part = uf.at[chunk_of(c, k, p)]
        return remote(part, part, s3.at[k, j - 1], d3.at[k, j - 1], chip(p))

    def pass_on(k, j):
        part = uf.at[chunk_of(c, k, lax.rem(q + nq - j, nq))]
        return remote(part, part, s4.at[k], d4.at[k], sibling)

    def passed(k):
        part = uf.at[rows_of(other, k)]
        return remote(part, part, s4.at[k], d4.at[k], sibling)

    for k in range(np_):
        own = borrowed(k, q)
        spread_all(k).wait_recv()
        for j in range(1, nq):
            own = own + r2[k, j - 1]
        uf[chunk_of(c, k, q), :] = own
        for j in range(1, nq):
            hand_out(k, j).start()
        pass_on(k, 0).start()
        if k == 0:
            ring_wait(0)
            ring_start(1)
    ring_wait(1)
    ring_start(2)

    def project(first):
        def body(i, carry):
            e = first + i
            base = pl.multiple_of(e * per, per)
            a = jnp.concatenate(split(uf[pl.ds(base, k1), :]), axis=0)
            b = jnp.concatenate(split(uf[pl.ds(base + k1, k1), :]), axis=0)
            down_part = dot(a, x_v[e], NN)
            up_part = dot(b, g_v[e], NN)
            at = pl.ds(pl.multiple_of(e * k1, k1), k1)
            high, low = split(down_part[:k1] + down_part[k1:])
            ha[0, at, :] = high
            ha[1, at, :] = low
            high, low = split(up_part[:k1] + up_part[k1:])
            hb[0, at, :] = high
            hb[1, at, :] = low
            return carry

        return body

    def combine(h, k):
        size = piece_e * k1
        at = pl.ds(pl.multiple_of((h * half_e + k * piece_e) * k1, k1), size)
        total = dot(ha[0, at, :], ra[...], NN) + dot(hb[0, at, :], rb[...], NN)
        total = total + (dot(ha[1, at, :], ra[...], NN) + dot(hb[1, at, :], rb[...], NN))
        total = total * scale
        t[0, at, :] = total[:, :128]
        t[1, at, :] = total[:, 128:]

    for k in range(np_):
        for j in range(1, nq):
            landed(k, j).wait_recv()
            pass_on(k, j).start()
        lax.fori_loop(0, piece_e, project(c * half_e + k * piece_e), 0)
        combine(c, k)
        passed(k).wait_recv()
        lax.fori_loop(0, piece_e, project(other * half_e + k * piece_e), 0)
        combine(other, k)
    for a in range(k1):
        cc, qq, al = (a // 2) % 2, a // 4, a % 2
        for side in range(2):
            ts[cc, qq, al * el : (al + 1) * el, side * 128 : (side + 1) * 128] = t[
                side, pl.ds(a, el, stride=k1), :
            ]

    swap = remote(ts.at[other], r3, s5.at[0], d5.at[0], sibling)
    swap.start()
    ring_wait(2)
    ring_start(3)
    swap.wait_recv()

    def scatter(j):
        p = lax.rem(q + j, nq)
        return remote(ts.at[c, p], r4.at[j - 1], s6.at[0], d6.at[0], chip(p))

    scatter_all = remote(r4, r4, s6.at[0], d6.at[0], chip(q))

    for j in range(1, nq):
        p = lax.rem(q + j, nq)
        ts[c, p] += r3[p]
        scatter(j).start()
    total = ts[c, q] + r3[q]

    ring_wait(3)

    def narrow(i, carry):
        vb[pl.ds(pl.multiple_of(i * vl, vl), vl), :] = vf[i].astype(BF16)
        return carry

    lax.fori_loop(0, nz, narrow, 0)
    ones = jnp.ones((16, vf.shape[2]), BF16)
    wide = vb[...].astype(F32)
    high, low = split(wide * wide)
    vq[0] = (dot(ones, high, NT) + dot(ones, low, NT))[0:1]

    def tally(j):
        p = lax.rem(m + j, nmp)
        return remote(vq.at[0], rq.at[j - 1], sq.at[0], dq.at[0], (dp, p))

    tally_all = remote(rq, rq, sq.at[0], dq.at[0], (dp, m))
    for j in range(1, nmp):
        tally(j).start()
    sc[...] = jnp.zeros_like(sc)

    scatter_all.wait_recv()
    for j in range(1, nq):
        total = total + r4[j - 1]
    tg[yh] = total

    def share(j):
        part = tg.at[yh]
        return remote(part, part, s7.at[0], d7.at[0], row(lax.rem(yh + j, nyh), m))

    shared = remote(tg.at[pl.ds(0, nyh - 1)], tg.at[pl.ds(0, nyh - 1)], s7.at[0], d7.at[0], row(yh, m))
    for j in range(1, nyh):
        share(j).start()
    tp_ref[:, 0:256] = total[0:el]
    tp_ref[:, 256:512] = total[el:te]
    if nyh > 1:
        shared.wait_recv()

    for y in range(nyh):
        for al in range(2):
            lt[y * el : (y + 1) * el, al * 256 : (al + 1) * 256] = tg[y, al * el : (al + 1) * el, :]
    train = lt[...]
    high, low = split(train)
    scores = dot(high, vb[...], NT) + dot(low, vb[...], NT)
    high, low = split(train * train)
    squares = (dot(ones, high, NT) + dot(ones, low, NT))[0:1]
    rows = nyh * el
    for i in range(nmp):
        sc[i, 0:er, :] = scores[i * er : (i + 1) * er, 0:hv]
        sc[i, er : 2 * er, :] = scores[i * er : (i + 1) * er, hv : 2 * hv]
        sc[i, 2 * er : 2 * er + 1, 0:rows] = squares

    def deal(j):
        p = lax.rem(m + j, nmp)
        return remote(sc.at[p], r5.at[j - 1], s8.at[0], d8.at[0], (dp, p))

    deal_all = remote(r5, r5, s8.at[0], d8.at[0], (dp, m))
    for j in range(1, nmp):
        deal(j).start()
    tally_all.wait_recv()
    norms = vq[0]
    for j in range(1, nmp):
        norms = norms + rq[j - 1]
    norms = lax.rsqrt(norms + EPSILON)
    row_id = lax.broadcasted_iota(jnp.int32, (8, hv), 0)
    lane_id = lax.broadcasted_iota(jnp.int32, (8, hv), 1)
    norms = jnp.where(row_id < er, norms[:, 0:hv], norms[:, hv : 2 * hv])
    deal_all.wait_recv()
    summed = sc[m]
    for j in range(1, nmp):
        summed = summed + r5[j - 1]

    cosines = summed * norms
    e_of = jnp.where(row_id < er, row_id, row_id - er)
    squares = jnp.sum(
        jnp.where(lane_id == m * er + e_of, summed[2 * er : 2 * er + 1, :], 0.0), axis=1, keepdims=True
    )
    weight = lax.rsqrt(squares + EPSILON) * root_k
    row_o = lax.broadcasted_iota(jnp.int32, (8, 128), 0)
    lane_o = lax.broadcasted_iota(jnp.int32, (8, 128), 1)
    placed = jnp.full((8, 128), LOWEST, F32)
    first_half = row_o < er
    e_of = jnp.where(first_half, row_o, row_o - er)
    for g in range(nz // 2):
        here = (lane_id >= g * vl) & (lane_id < (g + 1) * vl)
        best = jnp.max(jnp.where(here, cosines, LOWEST), axis=1, keepdims=True) * weight
        lane = e_of * nz + jnp.where(first_half, 0, nz // 2) + g
        placed = jnp.where((lane_o == lane) & (row_o < 2 * er), best, placed)
    mine = yh * nmp + m
    fp[mine] = jnp.max(placed, axis=0, keepdims=True)

    def tell(dy, dm):
        part = fp.at[mine]
        return remote(part, part, s9.at[0], d9.at[0], row(*neighbour(dy, dm)))

    told = remote(fp.at[pl.ds(0, len(others))], fp.at[pl.ds(0, len(others))], s9.at[0], d9.at[0], row(yh, m))
    for dy, dm in others:
        tell(dy, dm).start()
    told.wait_recv()
    best = fp[0:nmp]
    for y in range(1, nyh):
        best = jnp.maximum(best, fp[y * nmp : (y + 1) * nmp])
    fz[z] = best

    def publish(j):
        part = fz.at[z]
        return remote(part, part, s10.at[0], d10.at[0], column(lax.rem(z + j, nz)))

    published = remote(fz.at[pl.ds(0, nz - 1)], fz.at[pl.ds(0, nz - 1)], s10.at[0], d10.at[0], column(z))
    for j in range(1, nz):
        publish(j).start()

    for k in range(np_):
        lend(k).wait_send()
        spread_all(k).wait_send()
        passed(k).wait_send()
        for j in range(1, nq):
            hand_out(k, j).wait_send()
    swap.wait_send()
    scatter_all.wait_send()
    for step in range(steps):
        for copy in ring(step):
            copy.wait_send()
    tally_all.wait_send()
    if nyh > 1:
        shared.wait_send()
    deal_all.wait_send()
    told.wait_send()
    published.wait_recv()
    inf_ref[...] = fz[...]
    published.wait_send()


def on_device(nz, nyh, nq, np_, scale, root_k, *args):
    inputs, _, lengths, reducing, expanding, wseeds, rseeds, validation = args
    el, tokens, width = inputs.shape
    nmp = 2 * nq
    k1 = 2 * nmp
    vl, kl = validation.shape
    k2 = wseeds.shape[1]
    half_rows = el * k1
    piece_rows = half_rows // np_
    chunk = piece_rows // nq
    hv = nz * vl // 2
    dma = pltpu.SemaphoreType.DMA
    scratch = [
        pltpu.VMEM(inputs.shape, BF16),
        pltpu.VMEM(inputs.shape, BF16),
        pltpu.SMEM(lengths.shape, jnp.int32),
        pltpu.VMEM(reducing.shape, BF16),
        pltpu.VMEM(expanding.shape, BF16),
        pltpu.VMEM(wseeds.shape, jnp.int32),
        pltpu.VMEM(rseeds.shape, jnp.int32),
        pltpu.VMEM((8, 128), jnp.int32),
        pltpu.VMEM(validation.shape, BF16),
        pltpu.VMEM((2 * half_rows, tokens), F32),
        pltpu.VMEM((np_, piece_rows, tokens), F32),
        pltpu.VMEM((np_, nq - 1, chunk, tokens), F32),
        pltpu.VMEM((2 * half_rows, tokens), F32),
        pltpu.VMEM((width, k2), BF16),
        pltpu.VMEM((width, k2), BF16),
        pltpu.VMEM((2, el * k1, width), BF16),
        pltpu.VMEM((2, el * k1, width), BF16),
        pltpu.VMEM((2, el * k1, 128), F32),
        pltpu.VMEM((2, nq, 2 * el, k2), F32),
        pltpu.VMEM((nq, 2 * el, k2), F32),
        pltpu.VMEM((nq - 1, 2 * el, k2), F32),
        pltpu.VMEM((nyh, 2 * el, k2), F32),
        pltpu.VMEM((nyh * el, kl), F32),
        pltpu.VMEM((nz, vl, kl), F32),
        pltpu.VMEM((nz * vl, kl), BF16),
        pltpu.VMEM((1, 1, nz * vl), F32),
        pltpu.VMEM((nmp - 1, 1, nz * vl), F32),
        pltpu.VMEM((nmp, 8, hv), F32),
        pltpu.VMEM((nmp - 1, 8, hv), F32),
        pltpu.VMEM((nyh * nmp, 1, 128), F32),
        pltpu.VMEM((nz, nmp, 1, 128), F32),
        dma((2, 2 * np_)),
        dma((6,)),
    ]
    one = (1,)
    for count in (
        (np_,),
        (np_,),
        (np_, nq - 1),
        (np_,),
        one,
        one,
        one,
        (2, nz // 2),
        one,
        one,
        one,
        one,
    ):
        scratch += [dma(count), dma(count)]
    train_proj, best = pl.pallas_call(
        functools.partial(kernel, nz, nyh, nq, np_, scale, root_k),
        out_shape=(
            jax.ShapeDtypeStruct((el, kl), F32),
            jax.ShapeDtypeStruct((nz, nmp, 1, 128), F32),
        ),
        in_specs=[pl.BlockSpec(memory_space=pltpu.HBM)] * len(args),
        out_specs=[pl.BlockSpec(memory_space=pltpu.VMEM)] * 2,
        scratch_shapes=scratch,
        compiler_params=pltpu.CompilerParams(
            collective_id=0, has_side_effects=True, vmem_limit_bytes=48 * 1024 * 1024
        ),
    )(*[pltpu.with_memory_space_constraint(a, pltpu.HBM) for a in args])
    er = nyh * el // nmp
    influence = best.reshape(nz * nmp, 128)[:, : er * nz].reshape(nz * nmp * er, nz)
    return (train_proj, influence)


def solution(mesh, nyh=4, np_=2):
    ndp, nmp = mesh.shape["dp"], mesh.shape["mp"]
    nz, nq = ndp // nyh, nmp // 2
    width = nmp * 256
    scale = 1.0 / math.sqrt(2.0 * 128 * width * 256)
    root_k = math.sqrt(2 * nmp * 256)
    in_specs = (
        P("dp", None, "mp"),
        P("dp", None, "mp"),
        P("dp"),
        P(None, "mp"),
        P("mp", None),
        P(),
        P(),
        P("dp", "mp"),
    )
    return jax.shard_map(
        functools.partial(on_device, nz, nyh, nq, np_, scale, root_k),
        mesh=mesh,
        in_specs=in_specs,
        out_specs=(P("dp", "mp"), P()),
        check_vma=False,
    )
```

```python
import functools
import math

import jax
import jax.numpy as jnp
from jax import lax
from jax.experimental import pallas as pl
from jax.experimental.pallas import tpu as pltpu
from jax.sharding import PartitionSpec as P

MESH = pl.DeviceIdType.MESH
EPSILON = 1e-06
LOWEST = -3e38
F32 = jnp.float32
BF16 = jnp.bfloat16

NT = (((1,), (1,)), ((), ()))
NN = (((1,), (0,)), ((), ()))


def sign_of(seeds, columns):
    mixed = seeds + columns * 747796405
    for multiplier, distance in ((1103515245, 16), (1664525, 13), (22695477, 16)):
        mixed = mixed & 2147483647
        mixed = mixed ^ jnp.right_shift(mixed, distance)
        mixed = mixed * multiplier
    mixed = mixed & 2147483647
    parity = jnp.right_shift(mixed, 17) & 1
    return (1 - 2 * parity).astype(F32)


def dot(a, b, dims):
    return lax.dot_general(a, b, dims, preferred_element_type=F32)


def split(value):
    high = value.astype(BF16)
    return high, (value - high.astype(F32)).astype(BF16)


def kernel(nz, nyh, nq, np_, scale, root_k, *refs):
    (
        (x_ref, g_ref, len_ref, red_ref, exp_ref, wseed_ref, rseed_ref, val_ref, tp_ref, inf_ref),
        (x_v, g_v, len_v, red_v, exp_v, wseed_v, rseed_v, rpad, val_v, u, r1, r2, uf, ra, rb, ha, hb, t, ts, r3, r4),
        (tg, lt, vf, vb, vq, rq, sc, r5, fp, fz),
        (in_sem, small_sem, s1, d1, s2, d2, s3, d3, s4, d4, s5, d5, s6, d6, s7, d7, sv, dv, sq, dq, s8, d8, s9, d9, s10, d10, near),
    ) = refs[:10], refs[10:31], refs[31:41], refs[41:]
    nmp = 2 * nq
    el = x_v.shape[0]
    k1 = nmp * 2
    per = 2 * k1
    half_e = el // 2
    piece_e = half_e // np_
    half_rows = half_e * per
    piece_rows = piece_e * per
    chunk = piece_rows // nq
    tokens = x_v.shape[1]
    width = x_v.shape[2]
    vl = val_v.shape[0]
    te = 2 * el
    er = nyh * el // nmp
    hv = nz * vl // 2

    dp = lax.axis_index("dp")
    m = lax.axis_index("mp")
    q = lax.div(m, 2)
    c = lax.rem(m, 2)
    other = 1 - c
    z = lax.div(dp, nyh)
    yh = lax.rem(dp, nyh)
    sibling = (dp, 2 * q + other)

    nx = nq // 2
    ylo = lax.div(q, nx)
    x = lax.rem(q, nx)

    def ring_hops(d, n):
        return min(d, n - d)

    chips = [(dy, dx) for dy in range(2) for dx in range(nx) if (dy, dx) != (0, 0)]
    chips.sort(key=lambda d: -(d[0] + ring_hops(d[1], nx)))
    group = [(dy, dx, dc) for dy in range(2) for dx in range(nx) for dc in range(2) if (dy, dx, dc) != (0, 0, 0)]
    group.sort(key=lambda d: -(d[0] + ring_hops(d[1], nx)))
    planes = sorted(range(1, nz), key=lambda d: -ring_hops(d, nz))
    lines = sorted(range(1, nyh), key=lambda d: -ring_hops(d, nyh))

    def chip_at(shift, sign=1):
        return lax.rem(ylo + shift[0], 2) * nx + lax.rem(x + nx + sign * shift[1], nx)

    def member(shift):
        return 2 * chip_at(shift) + lax.rem(c + shift[2], 2)

    def chip(p):
        return (dp, 2 * p + c)

    def column(zz):
        return (zz * nyh + yh, m)

    def row(yy, mm):
        return (z * nyh + yy, mm)

    def remote(src, dst, send, recv, device):
        return pltpu.make_async_remote_copy(
            src_ref=src, dst_ref=dst, send_sem=send, recv_sem=recv, device_id=device, device_id_type=MESH
        )

    pieces = [(h, k) for h in (other, c) for k in range(np_)]

    def examples(h, k):
        return pl.ds(h * half_e + k * piece_e, piece_e)

    inputs = []
    for i, (h, k) in enumerate(pieces):
        inputs.append(
            (
                pltpu.make_async_copy(x_ref.at[examples(h, k)], x_v.at[examples(h, k)], in_sem.at[0, i]),
                pltpu.make_async_copy(g_ref.at[examples(h, k)], g_v.at[examples(h, k)], in_sem.at[1, i]),
            )
        )
    small = [
        pltpu.make_async_copy(a, b, small_sem.at[i])
        for i, (a, b) in enumerate(
            (
                (rseed_ref, rseed_v),
                (red_ref, red_v),
                (exp_ref, exp_v),
                (len_ref, len_v),
                (val_ref, val_v),
                (wseed_ref, wseed_v),
            )
        )
    ]
    for copy in small[:3] + list(inputs[0]):
        copy.start()

    barrier = pltpu.get_barrier_semaphore()
    shifts = (2, -2, 1, -1) if nz == 8 else (1, -1)
    sides = [j for j in (1, nyh - 1) if j < nyh][: nyh - 1]
    sides = sides[:1] if nyh == 2 else sides
    near_by = [sibling] + [chip(chip_at(shift)) for shift in chips]
    near_by += [column(lax.rem(z + nz + d, nz)) for d in shifts]
    near_by += [row(lax.rem(yh + j, nyh), m) for j in sides]
    for device in near_by:
        pl.semaphore_signal(barrier, inc=1, device_id=device, device_id_type=MESH)
    for copy in [small[3]] + [copy for pair in inputs[1:] for copy in pair] + small[4:]:
        copy.start()

    others = [(dyh, *shift) for dyh in range(nyh) for shift in [(0, 0, 0)] + group if (dyh, *shift) != (0, 0, 0, 0)]
    others.sort(key=lambda d: -(2 * ring_hops(d[0], nyh) + d[1] + ring_hops(d[2], nx)))

    def neighbour(dyh, *shift):
        return lax.rem(yh + dyh, nyh), member(shift)

    rpad[...] = jnp.zeros_like(rpad)
    small[0].wait()
    rpad[0:2, 0:k1] = rseed_v[...]
    ranks = lax.broadcasted_iota(jnp.int32, (128, 128), 0)
    left_a = sign_of(rpad[0:1, :], ranks).T[0:k1].astype(BF16)
    left_b = sign_of(rpad[1:2, :], ranks).T[0:k1].astype(BF16)
    small[1].wait()
    small[2].wait()
    p_out = jnp.concatenate(split(dot(left_a, exp_v[...], NT)), axis=0)
    p_in = jnp.concatenate(split(dot(left_b, red_v[...], NN)), axis=0)
    small[3].wait()

    lane_t = lax.broadcasted_iota(jnp.int32, (k1, tokens), 1)

    def sketch(first):
        def body(i, carry):
            e = first + i
            kept = lane_t < len_v[e]
            out = dot(p_out, g_v[e], NT)
            inn = dot(p_in, x_v[e], NT)
            base = pl.multiple_of(e * per, per)
            u[pl.ds(base, k1), :] = jnp.where(kept, out[:k1] + out[k1:], 0.0)
            u[pl.ds(base + k1, k1), :] = jnp.where(kept, inn[:k1] + inn[k1:], 0.0)
            return carry

        return body

    def sketch_piece(i):
        h, k = pieces[i]
        for copy in inputs[i]:
            copy.wait()
        lax.fori_loop(0, piece_e, sketch(h * half_e + k * piece_e), 0)

    def rows_of(h, k):
        return pl.ds(pl.multiple_of(h * half_rows + k * piece_rows, piece_rows), piece_rows)

    def chunk_of(h, k, p):
        return pl.ds(pl.multiple_of(h * half_rows + k * piece_rows + p * chunk, chunk), chunk)

    def lend(k):
        return remote(u.at[rows_of(other, k)], r1.at[k], s1.at[k], d1.at[k], sibling)

    def spread(k, i):
        p = chip_at(chips[i])
        return remote(u.at[chunk_of(c, k, p)], r2.at[k, i], s2.at[k], d2.at[k], chip(p))

    def spread_all(k):
        return remote(r2.at[k], r2.at[k], s2.at[k], d2.at[k], chip(q))

    def borrowed(k, p):
        return u[chunk_of(c, k, p), :] + r1[k, pl.ds(pl.multiple_of(p * chunk, chunk), chunk), :]

    def spread_piece(k):
        lend(k).wait_recv()
        for i, shift in enumerate(chips):
            p = chip_at(shift)
            u[chunk_of(c, k, p), :] = borrowed(k, p)
            spread(k, i).start()

    def along(i, offset, shift, part):
        at = lax.rem(z + nz + offset, nz)
        block = vf.at[at] if part is None else vf.at[at, pl.ds(part * (vl // 2), vl // 2)]
        return remote(block, block, sv.at[i], dv.at[i], column(lax.rem(z + nz + shift, nz)))

    def arrival(i, offset, shift, part):
        at = lax.rem(z + 2 * nz + offset - shift, nz)
        block = vf.at[at] if part is None else vf.at[at, pl.ds(part * (vl // 2), vl // 2)]
        return remote(block, block, sv.at[i], dv.at[i], column(lax.rem(z + nz - shift, nz)))

    first_hop = [(i, 0, d, None) for i, d in enumerate(shifts)]
    if nz == 8:
        second_hop = [(4, -2, 1, None), (5, 2, -1, None), (6, -2, 2, 0), (7, 2, -2, 1)]
    else:
        second_hop = [(2, -1, 1, 0), (3, 1, -1, 1)]

    early = min(np_, 2)
    for k in range(early):
        sketch_piece(k)
    pl.semaphore_wait(barrier, len(near_by))
    for k in range(np_):
        if k >= early:
            sketch_piece(k)
        lend(k).start()
    for j in sides:
        pl.semaphore_signal(near, inc=1, device_id=row(lax.rem(yh + j, nyh), m), device_id_type=MESH)
    small[4].wait()
    vf[z] = val_v[...].astype(F32)
    for hop in first_hop:
        along(*hop).start()
    for k in range(np_):
        sketch_piece(np_ + k)
        spread_piece(k)

    small[5].wait()
    columns = m * width + lax.broadcasted_iota(jnp.int32, (width, wseed_v.shape[1]), 0)
    ra[...] = sign_of(wseed_v[0:1, :], columns).astype(BF16)
    rb[...] = sign_of(wseed_v[1:2, :], columns).astype(BF16)

    def hand_out(k, i):
        part = uf.at[chunk_of(c, k, q)]
        return remote(part, part, s3.at[k, i], d3.at[k, i], chip(chip_at(chips[i])))

    def landed(k, i):
        p = chip_at(chips[i], -1)
        part = uf.at[chunk_of(c, k, p)]
        return remote(part, part, s3.at[k, i], d3.at[k, i], chip(p))

    def pass_on(k, p):
        part = uf.at[chunk_of(c, k, p)]
        return remote(part, part, s4.at[k], d4.at[k], sibling)

    def passed(k):
        part = uf.at[rows_of(other, k)]
        return remote(part, part, s4.at[k], d4.at[k], sibling)

    for k in range(np_):
        own = borrowed(k, q)
        spread_all(k).wait_recv()
        for j in range(1, nq):
            own = own + r2[k, j - 1]
        uf[chunk_of(c, k, q), :] = own
        for i in range(len(chips)):
            hand_out(k, i).start()
        pass_on(k, q).start()

    def ring_on():
        for hop in first_hop[:2]:
            arrival(*hop).wait_recv()
        for hop in second_hop:
            along(*hop).start()

    def project(first):
        def body(i, carry):
            e = first + i
            base = pl.multiple_of(e * per, per)
            a = jnp.concatenate(split(uf[pl.ds(base, k1), :]), axis=0)
            b = jnp.concatenate(split(uf[pl.ds(base + k1, k1), :]), axis=0)
            down_part = dot(a, x_v[e], NN)
            up_part = dot(b, g_v[e], NN)
            at = pl.ds(pl.multiple_of(e * k1, k1), k1)
            high, low = split(down_part[:k1] + down_part[k1:])
            ha[0, at, :] = high
            ha[1, at, :] = low
            high, low = split(up_part[:k1] + up_part[k1:])
            hb[0, at, :] = high
            hb[1, at, :] = low
            return carry

        return body

    def combine(h, k):
        size = piece_e * k1
        at = pl.ds(pl.multiple_of((h * half_e + k * piece_e) * k1, k1), size)
        total = dot(ha[0, at, :], ra[...], NN) + dot(hb[0, at, :], rb[...], NN)
        total = total + (dot(ha[1, at, :], ra[...], NN) + dot(hb[1, at, :], rb[...], NN))
        total = total * scale
        t[0, at, :] = total[:, :128]
        t[1, at, :] = total[:, 128:]

    def arrive(k):
        for i in reversed(range(len(chips))):
            landed(k, i).wait_recv()
            pass_on(k, chip_at(chips[i], -1)).start()

    def project_piece(h, k):
        lax.fori_loop(0, piece_e, project(h * half_e + k * piece_e), 0)
        combine(h, k)

    arrive(0)
    project_piece(c, 0)
    ring_on()
    for k in range(1, np_):
        arrive(k)
        passed(k - 1).wait_recv()
        project_piece(other, k - 1)
        project_piece(c, k)
    passed(np_ - 1).wait_recv()
    project_piece(other, np_ - 1)
    for a in range(k1):
        cc, qq, al = (a // 2) % 2, a // 4, a % 2
        for side in range(2):
            ts[cc, qq, al * el : (al + 1) * el, side * 128 : (side + 1) * 128] = t[
                side, pl.ds(a, el, stride=k1), :
            ]

    swap = remote(ts.at[other], r3, s5.at[0], d5.at[0], sibling)
    swap.start()
    swap.wait_recv()

    def scatter(i):
        p = chip_at(chips[i])
        return remote(ts.at[c, p], r4.at[i], s6.at[0], d6.at[0], chip(p))

    scatter_all = remote(r4, r4, s6.at[0], d6.at[0], chip(q))

    for i, shift in enumerate(chips):
        p = chip_at(shift)
        ts[c, p] += r3[p]
        scatter(i).start()
    total = ts[c, q] + r3[q]

    for hop in first_hop[2:] + second_hop:
        arrival(*hop).wait_recv()

    def narrow(i, carry):
        vb[pl.ds(pl.multiple_of(i * vl, vl), vl), :] = vf[i].astype(BF16)
        return carry

    lax.fori_loop(0, nz, narrow, 0)
    ones = jnp.ones((16, vf.shape[2]), BF16)
    wide = vb[...].astype(F32)
    high, low = split(wide * wide)
    vq[0] = (dot(ones, high, NT) + dot(ones, low, NT))[0:1]

    def tally(i):
        return remote(vq.at[0], rq.at[i], sq.at[0], dq.at[0], (dp, member(group[i])))

    tally_all = remote(rq, rq, sq.at[0], dq.at[0], (dp, m))
    for i in range(len(group)):
        tally(i).start()
    sc[...] = jnp.zeros_like(sc)

    scatter_all.wait_recv()
    for j in range(1, nq):
        total = total + r4[j - 1]
    tg[yh] = total

    def share(j):
        part = tg.at[yh]
        return remote(part, part, s7.at[0], d7.at[0], row(lax.rem(yh + j, nyh), m))

    shared = remote(tg.at[pl.ds(0, nyh - 1)], tg.at[pl.ds(0, nyh - 1)], s7.at[0], d7.at[0], row(yh, m))
    if sides:
        pl.semaphore_wait(near, len(sides))
    for j in lines:
        share(j).start()
    tp_ref[:, 0:256] = total[0:el]
    tp_ref[:, 256:512] = total[el:te]
    if nyh > 1:
        shared.wait_recv()

    for y in range(nyh):
        for al in range(2):
            lt[y * el : (y + 1) * el, al * 256 : (al + 1) * 256] = tg[y, al * el : (al + 1) * el, :]
    train = lt[...]
    high, low = split(train)
    scores = dot(high, vb[...], NT) + dot(low, vb[...], NT)
    high, low = split(train * train)
    squares = (dot(ones, high, NT) + dot(ones, low, NT))[0:1]
    rows = nyh * el
    for i in range(nmp):
        sc[i, 0:er, :] = scores[i * er : (i + 1) * er, 0:hv]
        sc[i, er : 2 * er, :] = scores[i * er : (i + 1) * er, hv : 2 * hv]
        sc[i, 2 * er : 2 * er + 1, 0:rows] = squares

    def deal(i):
        p = member(group[i])
        return remote(sc.at[p], r5.at[i], s8.at[0], d8.at[0], (dp, p))

    deal_all = remote(r5, r5, s8.at[0], d8.at[0], (dp, m))
    for i in range(len(group)):
        deal(i).start()
    tally_all.wait_recv()
    norms = vq[0]
    for j in range(1, nmp):
        norms = norms + rq[j - 1]
    norms = lax.rsqrt(norms + EPSILON)
    row_id = lax.broadcasted_iota(jnp.int32, (8, hv), 0)
    lane_id = lax.broadcasted_iota(jnp.int32, (8, hv), 1)
    norms = jnp.where(row_id < er, norms[:, 0:hv], norms[:, hv : 2 * hv])
    deal_all.wait_recv()
    summed = sc[m]
    for j in range(1, nmp):
        summed = summed + r5[j - 1]

    cosines = summed * norms
    e_of = jnp.where(row_id < er, row_id, row_id - er)
    squares = jnp.sum(
        jnp.where(lane_id == m * er + e_of, summed[2 * er : 2 * er + 1, :], 0.0), axis=1, keepdims=True
    )
    weight = lax.rsqrt(squares + EPSILON) * root_k
    row_o = lax.broadcasted_iota(jnp.int32, (8, 128), 0)
    lane_o = lax.broadcasted_iota(jnp.int32, (8, 128), 1)
    placed = jnp.full((8, 128), LOWEST, F32)
    first_half = row_o < er
    e_of = jnp.where(first_half, row_o, row_o - er)
    for g in range(nz // 2):
        here = (lane_id >= g * vl) & (lane_id < (g + 1) * vl)
        best = jnp.max(jnp.where(here, cosines, LOWEST), axis=1, keepdims=True) * weight
        lane = e_of * nz + jnp.where(first_half, 0, nz // 2) + g
        placed = jnp.where((lane_o == lane) & (row_o < 2 * er), best, placed)
    mine = yh * nmp + m
    fp[mine] = jnp.max(placed, axis=0, keepdims=True)

    def tell(shift):
        part = fp.at[mine]
        return remote(part, part, s9.at[0], d9.at[0], row(*neighbour(*shift)))

    told = remote(fp.at[pl.ds(0, len(others))], fp.at[pl.ds(0, len(others))], s9.at[0], d9.at[0], row(yh, m))
    for shift in others:
        tell(shift).start()
    told.wait_recv()
    best = fp[0:nmp]
    for y in range(1, nyh):
        best = jnp.maximum(best, fp[y * nmp : (y + 1) * nmp])
    fz[z] = best

    def publish(j):
        part = fz.at[z]
        return remote(part, part, s10.at[0], d10.at[0], column(lax.rem(z + j, nz)))

    published = remote(fz.at[pl.ds(0, nz - 1)], fz.at[pl.ds(0, nz - 1)], s10.at[0], d10.at[0], column(z))
    for j in planes:
        publish(j).start()

    for k in range(np_):
        lend(k).wait_send()
        spread_all(k).wait_send()
        passed(k).wait_send()
        for i in range(len(chips)):
            hand_out(k, i).wait_send()
    swap.wait_send()
    scatter_all.wait_send()
    for hop in first_hop + second_hop:
        along(*hop).wait_send()
    tally_all.wait_send()
    if nyh > 1:
        shared.wait_send()
    deal_all.wait_send()
    told.wait_send()
    published.wait_recv()
    inf_ref[...] = fz[...]
    published.wait_send()


def on_device(nz, nyh, nq, np_, scale, root_k, *args):
    inputs, _, lengths, reducing, expanding, wseeds, rseeds, validation = args
    el, tokens, width = inputs.shape
    nmp = 2 * nq
    k1 = 2 * nmp
    vl, kl = validation.shape
    k2 = wseeds.shape[1]
    half_rows = el * k1
    piece_rows = half_rows // np_
    chunk = piece_rows // nq
    hv = nz * vl // 2
    dma = pltpu.SemaphoreType.DMA
    scratch = [
        pltpu.VMEM(inputs.shape, BF16),
        pltpu.VMEM(inputs.shape, BF16),
        pltpu.SMEM(lengths.shape, jnp.int32),
        pltpu.VMEM(reducing.shape, BF16),
        pltpu.VMEM(expanding.shape, BF16),
        pltpu.VMEM(wseeds.shape, jnp.int32),
        pltpu.VMEM(rseeds.shape, jnp.int32),
        pltpu.VMEM((8, 128), jnp.int32),
        pltpu.VMEM(validation.shape, BF16),
        pltpu.VMEM((2 * half_rows, tokens), F32),
        pltpu.VMEM((np_, piece_rows, tokens), F32),
        pltpu.VMEM((np_, nq - 1, chunk, tokens), F32),
        pltpu.VMEM((2 * half_rows, tokens), F32),
        pltpu.VMEM((width, k2), BF16),
        pltpu.VMEM((width, k2), BF16),
        pltpu.VMEM((2, el * k1, width), BF16),
        pltpu.VMEM((2, el * k1, width), BF16),
        pltpu.VMEM((2, el * k1, 128), F32),
        pltpu.VMEM((2, nq, 2 * el, k2), F32),
        pltpu.VMEM((nq, 2 * el, k2), F32),
        pltpu.VMEM((nq - 1, 2 * el, k2), F32),
        pltpu.VMEM((nyh, 2 * el, k2), F32),
        pltpu.VMEM((nyh * el, kl), F32),
        pltpu.VMEM((nz, vl, kl), F32),
        pltpu.VMEM((nz * vl, kl), BF16),
        pltpu.VMEM((1, 1, nz * vl), F32),
        pltpu.VMEM((nmp - 1, 1, nz * vl), F32),
        pltpu.VMEM((nmp, 8, hv), F32),
        pltpu.VMEM((nmp - 1, 8, hv), F32),
        pltpu.VMEM((nyh * nmp, 1, 128), F32),
        pltpu.VMEM((nz, nmp, 1, 128), F32),
        dma((2, 2 * np_)),
        dma((6,)),
    ]
    one = (1,)
    for count in (
        (np_,),
        (np_,),
        (np_, nq - 1),
        (np_,),
        one,
        one,
        one,
        (nz,),
        one,
        one,
        one,
        one,
    ):
        scratch += [dma(count), dma(count)]
    scratch.append(pltpu.SemaphoreType.REGULAR)
    train_proj, best = pl.pallas_call(
        functools.partial(kernel, nz, nyh, nq, np_, scale, root_k),
        out_shape=(
            jax.ShapeDtypeStruct((el, kl), F32),
            jax.ShapeDtypeStruct((nz, nmp, 1, 128), F32),
        ),
        in_specs=[pl.BlockSpec(memory_space=pltpu.HBM)] * len(args),
        out_specs=[pl.BlockSpec(memory_space=pltpu.VMEM)] * 2,
        scratch_shapes=scratch,
        compiler_params=pltpu.CompilerParams(
            collective_id=0, has_side_effects=True, vmem_limit_bytes=48 * 1024 * 1024
        ),
    )(*[pltpu.with_memory_space_constraint(a, pltpu.HBM) for a in args])
    er = nyh * el // nmp
    influence = best.reshape(nz * nmp, 128)[:, : er * nz].reshape(nz * nmp * er, nz)
    return (train_proj, influence)


def solution(mesh, nyh=4, np_=2):
    ndp, nmp = mesh.shape["dp"], mesh.shape["mp"]
    nz, nq = ndp // nyh, nmp // 2
    width = nmp * 256
    scale = 1.0 / math.sqrt(2.0 * 128 * width * 256)
    root_k = math.sqrt(2 * nmp * 256)
    in_specs = (
        P("dp", None, "mp"),
        P("dp", None, "mp"),
        P("dp"),
        P(None, "mp"),
        P("mp", None),
        P(),
        P(),
        P("dp", "mp"),
    )
    return jax.shard_map(
        functools.partial(on_device, nz, nyh, nq, np_, scale, root_k),
        mesh=mesh,
        in_specs=in_specs,
        out_specs=(P("dp", "mp"), P()),
        check_vma=False,
    )
```

```python
import functools
import math

import jax
import jax.numpy as jnp
from jax import lax
from jax.experimental import pallas as pl
from jax.experimental.pallas import tpu as pltpu
from jax.sharding import PartitionSpec as P

MESH = pl.DeviceIdType.MESH
EPSILON = 1e-06
LOWEST = -3e38
F32 = jnp.float32
BF16 = jnp.bfloat16

NT = (((1,), (1,)), ((), ()))
NN = (((1,), (0,)), ((), ()))


def sign_of(seeds, columns):
    mixed = seeds + columns * 747796405
    for multiplier, distance in ((1103515245, 16), (1664525, 13), (22695477, 16)):
        mixed = mixed & 2147483647
        mixed = mixed ^ jnp.right_shift(mixed, distance)
        mixed = mixed * multiplier
    mixed = mixed & 2147483647
    parity = jnp.right_shift(mixed, 17) & 1
    return (1 - 2 * parity).astype(F32)


def dot(a, b, dims):
    return lax.dot_general(a, b, dims, preferred_element_type=F32)


def split(value):
    high = value.astype(BF16)
    return high, (value - high.astype(F32)).astype(BF16)


def kernel(nz, nyh, nq, np_, scale, root_k, *refs):
    (
        (x_ref, g_ref, len_ref, red_ref, exp_ref, wseed_ref, rseed_ref, val_ref, tp_ref, inf_ref),
        (x_v, g_v, len_v, red_v, exp_v, wseed_v, rseed_v, rpad, val_v, u, r1, r2, uf, ra, rb, ha, hb, t, ts, r4, xf, xr, xs),
        (tg, lt, vf, vb, vq, rq, sc, r5, fp, fz),
        (in_sem, small_sem, s1, d1, s2, d2, s3, d3, s4, d4, s6, d6, s7, d7, sv, dv, sq, dq, s8, d8, s9, d9, s10, d10, near),
    ) = refs[:10], refs[10:33], refs[33:43], refs[43:]
    nmp = 2 * nq
    el = x_v.shape[0]
    k1 = nmp * 2
    per = 2 * k1
    half_e = el // 2
    piece_e = half_e // np_
    half_rows = half_e * per
    piece_rows = piece_e * per
    chunk = piece_rows // nq
    tokens = x_v.shape[1]
    width = x_v.shape[2]
    vl = val_v.shape[0]
    te = 2 * el
    er = nyh * el // nmp
    hv = nz * vl // 2

    dp = lax.axis_index("dp")
    m = lax.axis_index("mp")
    q = lax.div(m, 2)
    c = lax.rem(m, 2)
    other = 1 - c
    z = lax.div(dp, nyh)
    yh = lax.rem(dp, nyh)
    sibling = (dp, 2 * q + other)

    nx = nq // 2
    ylo = lax.div(q, nx)
    x = lax.rem(q, nx)

    def ring_hops(d, n):
        return min(d, n - d)

    chips = [(dy, dx) for dy in range(2) for dx in range(nx) if (dy, dx) != (0, 0)]
    chips.sort(key=lambda d: -(d[0] + ring_hops(d[1], nx)))
    group = [(dy, dx, dc) for dy in range(2) for dx in range(nx) for dc in range(2) if (dy, dx, dc) != (0, 0, 0)]
    group.sort(key=lambda d: -(d[0] + ring_hops(d[1], nx)))
    planes = sorted(range(1, nz), key=lambda d: -ring_hops(d, nz))
    lines = sorted(range(1, nyh), key=lambda d: -ring_hops(d, nyh))

    def chip_at(shift, sign=1):
        return lax.rem(ylo + shift[0], 2) * nx + lax.rem(x + nx + sign * shift[1], nx)

    def member(shift):
        return 2 * chip_at(shift) + lax.rem(c + shift[2], 2)

    def chip(p):
        return (dp, 2 * p + c)

    def column(zz):
        return (zz * nyh + yh, m)

    def row(yy, mm):
        return (z * nyh + yy, mm)

    def remote(src, dst, send, recv, device):
        return pltpu.make_async_remote_copy(
            src_ref=src, dst_ref=dst, send_sem=send, recv_sem=recv, device_id=device, device_id_type=MESH
        )

    pieces = [(h, k) for h in (other, c) for k in range(np_)]

    def examples(h, k):
        return pl.ds(h * half_e + k * piece_e, piece_e)

    inputs = []
    for i, (h, k) in enumerate(pieces):
        inputs.append(
            (
                pltpu.make_async_copy(x_ref.at[examples(h, k)], x_v.at[examples(h, k)], in_sem.at[0, i]),
                pltpu.make_async_copy(g_ref.at[examples(h, k)], g_v.at[examples(h, k)], in_sem.at[1, i]),
            )
        )
    small = [
        pltpu.make_async_copy(a, b, small_sem.at[i])
        for i, (a, b) in enumerate(
            (
                (rseed_ref, rseed_v),
                (red_ref, red_v),
                (exp_ref, exp_v),
                (len_ref, len_v),
                (val_ref, val_v),
                (wseed_ref, wseed_v),
            )
        )
    ]
    for copy in small[:3] + list(inputs[0]):
        copy.start()

    barrier = pltpu.get_barrier_semaphore()
    shifts = (2, -2, 1, -1) if nz == 8 else (1, -1)
    sides = [j for j in (1, nyh - 1) if j < nyh][: nyh - 1]
    sides = sides[:1] if nyh == 2 else sides
    near_by = [sibling] + [chip(chip_at(shift)) for shift in chips]
    near_by += [column(lax.rem(z + nz + d, nz)) for d in shifts]
    near_by += [row(lax.rem(yh + j, nyh), m) for j in sides]
    for device in near_by:
        pl.semaphore_signal(barrier, inc=1, device_id=device, device_id_type=MESH)
    for copy in [small[3]] + [copy for pair in inputs[1:] for copy in pair] + small[4:]:
        copy.start()

    others = [(dyh, *shift) for dyh in range(nyh) for shift in [(0, 0, 0)] + group if (dyh, *shift) != (0, 0, 0, 0)]
    others.sort(key=lambda d: -(2 * ring_hops(d[0], nyh) + d[1] + ring_hops(d[2], nx)))

    def neighbour(dyh, *shift):
        return lax.rem(yh + dyh, nyh), member(shift)

    rpad[...] = jnp.zeros_like(rpad)
    small[0].wait()
    rpad[0:2, 0:k1] = rseed_v[...]
    ranks = lax.broadcasted_iota(jnp.int32, (128, 128), 0)
    left_a = sign_of(rpad[0:1, :], ranks).T[0:k1].astype(BF16)
    left_b = sign_of(rpad[1:2, :], ranks).T[0:k1].astype(BF16)
    small[1].wait()
    small[2].wait()
    p_out = jnp.concatenate(split(dot(left_a, exp_v[...], NT)), axis=0)
    p_in = jnp.concatenate(split(dot(left_b, red_v[...], NN)), axis=0)
    small[3].wait()

    lane_t = lax.broadcasted_iota(jnp.int32, (k1, tokens), 1)

    def sketch(first):
        def body(i, carry):
            e = first + i
            kept = lane_t < len_v[e]
            out = dot(p_out, g_v[e], NT)
            inn = dot(p_in, x_v[e], NT)
            base = pl.multiple_of(e * per, per)
            u[pl.ds(base, k1), :] = jnp.where(kept, out[:k1] + out[k1:], 0.0)
            u[pl.ds(base + k1, k1), :] = jnp.where(kept, inn[:k1] + inn[k1:], 0.0)
            return carry

        return body

    def sketch_piece(i):
        h, k = pieces[i]
        for copy in inputs[i]:
            copy.wait()
        lax.fori_loop(0, piece_e, sketch(h * half_e + k * piece_e), 0, unroll=True)

    def rows_of(h, k):
        return pl.ds(pl.multiple_of(h * half_rows + k * piece_rows, piece_rows), piece_rows)

    def chunk_of(h, k, p):
        return pl.ds(pl.multiple_of(h * half_rows + k * piece_rows + p * chunk, chunk), chunk)

    def lend(k):
        return remote(u.at[rows_of(other, k)], r1.at[k], s1.at[k], d1.at[k], sibling)

    def spread(k, i):
        p = chip_at(chips[i])
        return remote(u.at[chunk_of(c, k, p)], r2.at[k, i], s2.at[k], d2.at[k], chip(p))

    def spread_all(k):
        return remote(r2.at[k], r2.at[k], s2.at[k], d2.at[k], chip(q))

    def borrowed(k, p):
        return u[chunk_of(c, k, p), :] + r1[k, pl.ds(pl.multiple_of(p * chunk, chunk), chunk), :]

    def spread_piece(k):
        lend(k).wait_recv()
        for i, shift in enumerate(chips):
            p = chip_at(shift)
            u[chunk_of(c, k, p), :] = borrowed(k, p)
            spread(k, i).start()

    def along(i, offset, shift, part):
        at = lax.rem(z + nz + offset, nz)
        block = vf.at[at] if part is None else vf.at[at, pl.ds(part * (vl // 2), vl // 2)]
        return remote(block, block, sv.at[i], dv.at[i], column(lax.rem(z + nz + shift, nz)))

    def arrival(i, offset, shift, part):
        at = lax.rem(z + 2 * nz + offset - shift, nz)
        block = vf.at[at] if part is None else vf.at[at, pl.ds(part * (vl // 2), vl // 2)]
        return remote(block, block, sv.at[i], dv.at[i], column(lax.rem(z + nz - shift, nz)))

    first_hop = [(i, 0, d, None) for i, d in enumerate(shifts)]
    if nz == 8:
        second_hop = [(4, -2, 1, None), (5, 2, -1, None), (6, -2, 2, 0), (7, 2, -2, 1)]
    else:
        second_hop = [(2, -1, 1, 0), (3, 1, -1, 1)]

    for k in range(np_ + 1):
        sketch_piece(k)
    pl.semaphore_wait(barrier, len(near_by))
    for k in range(np_):
        lend(k).start()
    for j in sides:
        pl.semaphore_signal(near, inc=1, device_id=row(lax.rem(yh + j, nyh), m), device_id_type=MESH)
    small[4].wait()
    vf[z] = val_v[...].astype(F32)
    for hop in first_hop:
        along(*hop).start()
    for k in range(np_):
        if k:
            sketch_piece(np_ + k)
        spread_piece(k)

    def trade(k, side):
        part = pl.ds(k * piece_e, piece_e)
        return remote(xf.at[side, part], xr.at[side, part], s4.at[k, side], d4.at[k, side], sibling)

    for k in range(np_):
        for side, tokens_v in enumerate((x_v, g_v)):

            def widen(i, carry, side=side, tokens_v=tokens_v, k=k):
                xf[side, k * piece_e + i] = tokens_v[other * half_e + k * piece_e + i].astype(F32)
                return carry

            lax.fori_loop(0, piece_e, widen, 0)
            trade(k, side).start()

    small[5].wait()
    for s, device in enumerate((m, 2 * q + other)):
        columns = device * width + lax.broadcasted_iota(jnp.int32, (width, wseed_v.shape[1]), 0)
        ra[s] = sign_of(wseed_v[0:1, :], columns).astype(BF16)
        rb[s] = sign_of(wseed_v[1:2, :], columns).astype(BF16)

    def hand_out(k, i):
        part = uf.at[chunk_of(0, k, q)]
        return remote(part, part, s3.at[k], d3.at[k], chip(chip_at(chips[i])))

    def landed(k):
        return remote(r2.at[k], r2.at[k], s3.at[k], d3.at[k], chip(q))

    for k in range(np_):
        own = borrowed(k, q)
        spread_all(k).wait_recv()
        for j in range(1, nq):
            own = own + r2[k, j - 1]
        uf[chunk_of(0, k, q), :] = own
        for i in range(len(chips)):
            hand_out(k, i).start()

    def ring_on():
        for hop in first_hop[:2]:
            arrival(*hop).wait_recv()
        for hop in second_hop:
            along(*hop).start()

    for k in range(np_):
        for side in range(2):
            trade(k, side).wait_recv()

            def narrow_tokens(i, carry, side=side, k=k):
                xs[side, k * piece_e + i] = xr[side, k * piece_e + i].astype(BF16)
                return carry

            lax.fori_loop(0, piece_e, narrow_tokens, 0)
    ring_on()

    def project(i, carry):
        base = i * per
        a = jnp.concatenate(split(uf[pl.ds(base, k1), :]), axis=0)
        b = jnp.concatenate(split(uf[pl.ds(base + k1, k1), :]), axis=0)
        at = pl.ds(i * k1, k1)
        e = c * half_e + i
        for s, (xe, ge) in enumerate(((x_v[e], g_v[e]), (xs[0, i], xs[1, i]))):
            down_part = dot(a, xe, NN)
            up_part = dot(b, ge, NN)
            for h, part in ((ha, down_part), (hb, up_part)):
                high, low = split(part[:k1] + part[k1:])
                h[s, 0, at, :] = high
                h[s, 1, at, :] = low
        return carry

    def combine(k):
        size = piece_e * k1
        at = pl.ds(k * size, size)
        total = 0.0
        for s in range(2):
            for h, r in ((ha, ra), (hb, rb)):
                total = total + dot(jnp.concatenate([h[s, 0, at, :], h[s, 1, at, :]], axis=0), r[s], NN)
        total = (total[:size] + total[size:]) * scale
        t[0, at, :] = total[:, :128]
        t[1, at, :] = total[:, 128:]

    for k in range(np_):
        landed(k).wait_recv()
        for i in range(piece_e):
            project(k * piece_e + i, 0)
        combine(k)
    for a in range(k1):
        for side in range(2):
            at = side * 2 * half_e + (a % 2) * half_e
            ts[a // 2, at : at + half_e, :] = t[side, pl.ds(a, half_e, stride=k1), :]

    def scatter(i):
        p = member(group[i])
        return remote(ts.at[p], r4.at[i], s6.at[0], d6.at[0], (dp, p))

    scatter_all = remote(r4, r4, s6.at[0], d6.at[0], (dp, m))

    for i in range(len(group)):
        scatter(i).start()

    for hop in first_hop[2:] + second_hop:
        arrival(*hop).wait_recv()

    def narrow(i, carry):
        vb[pl.ds(pl.multiple_of(i * vl, vl), vl), :] = vf[i].astype(BF16)
        return carry

    lax.fori_loop(0, nz, narrow, 0)
    ones = jnp.ones((16, vf.shape[2]), BF16)
    wide = vb[...].astype(F32)
    high, low = split(wide * wide)
    vq[0] = (dot(ones, high, NT) + dot(ones, low, NT))[0:1]

    def tally(i):
        return remote(vq.at[0], rq.at[i], sq.at[0], dq.at[0], (dp, member(group[i])))

    tally_all = remote(rq, rq, sq.at[0], dq.at[0], (dp, m))
    for i in range(len(group)):
        tally(i).start()
    sc[...] = jnp.zeros_like(sc)

    scatter_all.wait_recv()
    mine, theirs = ts[m], 0.0
    for i, shift in enumerate(group):
        if shift[2]:
            theirs = theirs + r4[i]
        else:
            mine = mine + r4[i]
    tg[yh, 0:te] = jnp.where(c == 0, mine, theirs)
    tg[yh, te : 2 * te] = jnp.where(c == 0, theirs, mine)

    def share(j):
        part = tg.at[yh]
        return remote(part, part, s7.at[0], d7.at[0], row(lax.rem(yh + j, nyh), m))

    shared = remote(tg.at[pl.ds(0, nyh - 1)], tg.at[pl.ds(0, nyh - 1)], s7.at[0], d7.at[0], row(yh, m))
    if sides:
        pl.semaphore_wait(near, len(sides))
    for j in lines:
        share(j).start()

    def unfold(target, first, y):
        for h in range(2):
            for side in range(2):
                for al in range(2):
                    at = h * te + side * el + al * half_e
                    lanes = al * 256 + side * 128
                    target[first + h * half_e : first + (h + 1) * half_e, lanes : lanes + 128] = tg[y, at : at + half_e, :]

    unfold(tp_ref, 0, yh)
    if nyh > 1:
        shared.wait_recv()

    for y in range(nyh):
        unfold(lt, y * el, y)
    train = lt[...]
    rows = nyh * el
    scores = dot(jnp.concatenate(split(train), axis=0), vb[...], NT)
    scores = scores[:rows] + scores[rows:]
    high, low = split(train * train)
    squares = (dot(ones, high, NT) + dot(ones, low, NT))[0:1]
    for i in range(nmp):
        sc[i, 0:er, :] = scores[i * er : (i + 1) * er, 0:hv]
        sc[i, er : 2 * er, :] = scores[i * er : (i + 1) * er, hv : 2 * hv]
        sc[i, 2 * er : 2 * er + 1, 0:rows] = squares

    def deal(i):
        p = member(group[i])
        return remote(sc.at[p], r5.at[i], s8.at[0], d8.at[0], (dp, p))

    deal_all = remote(r5, r5, s8.at[0], d8.at[0], (dp, m))
    for i in range(len(group)):
        deal(i).start()
    tally_all.wait_recv()
    norms = vq[0]
    for j in range(1, nmp):
        norms = norms + rq[j - 1]
    norms = lax.rsqrt(norms + EPSILON)
    row_id = lax.broadcasted_iota(jnp.int32, (8, hv), 0)
    lane_id = lax.broadcasted_iota(jnp.int32, (8, hv), 1)
    norms = jnp.where(row_id < er, norms[:, 0:hv], norms[:, hv : 2 * hv])
    deal_all.wait_recv()
    summed = sc[m]
    for j in range(1, nmp):
        summed = summed + r5[j - 1]

    cosines = summed * norms
    e_of = jnp.where(row_id < er, row_id, row_id - er)
    squares = jnp.sum(
        jnp.where(lane_id == m * er + e_of, summed[2 * er : 2 * er + 1, :], 0.0), axis=1, keepdims=True
    )
    weight = lax.rsqrt(squares + EPSILON) * root_k
    row_o = lax.broadcasted_iota(jnp.int32, (8, 128), 0)
    lane_o = lax.broadcasted_iota(jnp.int32, (8, 128), 1)
    placed = jnp.full((8, 128), LOWEST, F32)
    start = lax.rem(m, 4) * (er * nz)
    first_half = row_o < er
    e_of = jnp.where(first_half, row_o, row_o - er)
    for g in range(nz // 2):
        here = (lane_id >= g * vl) & (lane_id < (g + 1) * vl)
        best = jnp.max(jnp.where(here, cosines, LOWEST), axis=1, keepdims=True) * weight
        lane = start + e_of * nz + jnp.where(first_half, 0, nz // 2) + g
        placed = jnp.where((lane_o == lane) & (row_o < 2 * er), best, placed)
    place = yh * nmp + m
    fp[place] = jnp.max(placed, axis=0, keepdims=True)

    def tell(shift):
        part = fp.at[place]
        return remote(part, part, s9.at[0], d9.at[0], row(*neighbour(*shift)))

    told = remote(fp.at[pl.ds(0, len(others))], fp.at[pl.ds(0, len(others))], s9.at[0], d9.at[0], row(yh, m))
    for shift in others:
        tell(shift).start()
    told.wait_recv()
    best = [fp[4 * i : 4 * i + 4] for i in range(nyh * nmp // 4)]
    for i in range(nmp // 4):
        fz[z, i] = jnp.max(functools.reduce(jnp.maximum, best[i :: nmp // 4]), axis=0)

    def publish(j):
        part = fz.at[z]
        return remote(part, part, s10.at[0], d10.at[0], column(lax.rem(z + j, nz)))

    published = remote(fz.at[pl.ds(0, nz - 1)], fz.at[pl.ds(0, nz - 1)], s10.at[0], d10.at[0], column(z))
    for j in planes:
        publish(j).start()

    for k in range(np_):
        lend(k).wait_send()
        spread_all(k).wait_send()
        landed(k).wait_send()
        for side in range(2):
            trade(k, side).wait_send()
    scatter_all.wait_send()
    for hop in first_hop + second_hop:
        along(*hop).wait_send()
    tally_all.wait_send()
    if nyh > 1:
        shared.wait_send()
    deal_all.wait_send()
    told.wait_send()
    published.wait_recv()
    inf_ref[...] = fz[...]
    published.wait_send()


def on_device(nz, nyh, nq, np_, scale, root_k, *args):
    inputs, _, lengths, reducing, expanding, wseeds, rseeds, validation = args
    el, tokens, width = inputs.shape
    nmp = 2 * nq
    k1 = 2 * nmp
    vl, kl = validation.shape
    k2 = wseeds.shape[1]
    half_rows = el * k1
    piece_rows = half_rows // np_
    chunk = piece_rows // nq
    hv = nz * vl // 2
    dma = pltpu.SemaphoreType.DMA
    scratch = [
        pltpu.VMEM(inputs.shape, BF16),
        pltpu.VMEM(inputs.shape, BF16),
        pltpu.SMEM(lengths.shape, jnp.int32),
        pltpu.VMEM(reducing.shape, BF16),
        pltpu.VMEM(expanding.shape, BF16),
        pltpu.VMEM(wseeds.shape, jnp.int32),
        pltpu.VMEM(rseeds.shape, jnp.int32),
        pltpu.VMEM((8, 128), jnp.int32),
        pltpu.VMEM(validation.shape, BF16),
        pltpu.VMEM((2 * half_rows, tokens), F32),
        pltpu.VMEM((np_, piece_rows, tokens), F32),
        pltpu.VMEM((np_, nq - 1, chunk, tokens), F32),
        pltpu.VMEM((half_rows, tokens), F32),
        pltpu.VMEM((2, width, k2), BF16),
        pltpu.VMEM((2, width, k2), BF16),
        pltpu.VMEM((2, 2, el * k1 // 2, width), BF16),
        pltpu.VMEM((2, 2, el * k1 // 2, width), BF16),
        pltpu.VMEM((2, el * k1 // 2, 128), F32),
        pltpu.VMEM((nmp, 2 * el, 128), F32),
        pltpu.VMEM((nmp - 1, 2 * el, 128), F32),
        pltpu.VMEM((2, el // 2, tokens, width), F32),
        pltpu.VMEM((2, el // 2, tokens, width), F32),
        pltpu.VMEM((2, el // 2, tokens, width), BF16),
        pltpu.VMEM((nyh, 4 * el, 128), F32),
        pltpu.VMEM((nyh * el, kl), F32),
        pltpu.VMEM((nz, vl, kl), F32),
        pltpu.VMEM((nz * vl, kl), BF16),
        pltpu.VMEM((1, 1, nz * vl), F32),
        pltpu.VMEM((nmp - 1, 1, nz * vl), F32),
        pltpu.VMEM((nmp, 8, hv), F32),
        pltpu.VMEM((nmp - 1, 8, hv), F32),
        pltpu.VMEM((nyh * nmp, 1, 128), F32),
        pltpu.VMEM((nz, nmp // 4, 1, 128), F32),
        dma((2, 2 * np_)),
        dma((6,)),
    ]
    one = (1,)
    for count in (
        (np_,),
        (np_,),
        (np_,),
        (np_, 2),
        one,
        one,
        (nz,),
        one,
        one,
        one,
        one,
    ):
        scratch += [dma(count), dma(count)]
    scratch.append(pltpu.SemaphoreType.REGULAR)
    train_proj, best = pl.pallas_call(
        functools.partial(kernel, nz, nyh, nq, np_, scale, root_k),
        out_shape=(
            jax.ShapeDtypeStruct((el, kl), F32),
            jax.ShapeDtypeStruct((nz, nmp // 4, 1, 128), F32),
        ),
        in_specs=[pl.BlockSpec(memory_space=pltpu.HBM)] * len(args),
        out_specs=[pl.BlockSpec(memory_space=pltpu.VMEM)] * 2,
        scratch_shapes=scratch,
        compiler_params=pltpu.CompilerParams(
            collective_id=0, has_side_effects=True, vmem_limit_bytes=48 * 1024 * 1024
        ),
    )(*[pltpu.with_memory_space_constraint(a, pltpu.HBM) for a in args])
    er = nyh * el // nmp
    influence = best.reshape(nz * nmp // 4, 128)[:, : 4 * er * nz].reshape(nz * nmp * er, nz)
    return (train_proj, influence)


def solution(mesh, nyh=4, np_=2):
    ndp, nmp = mesh.shape["dp"], mesh.shape["mp"]
    nz, nq = ndp // nyh, nmp // 2
    width = nmp * 256
    scale = 1.0 / math.sqrt(2.0 * 128 * width * 256)
    root_k = math.sqrt(2 * nmp * 256)
    in_specs = (
        P("dp", None, "mp"),
        P("dp", None, "mp"),
        P("dp"),
        P(None, "mp"),
        P("mp", None),
        P(),
        P(),
        P("dp", "mp"),
    )
    return jax.shard_map(
        functools.partial(on_device, nz, nyh, nq, np_, scale, root_k),
        mesh=mesh,
        in_specs=in_specs,
        out_specs=(P("dp", "mp"), P()),
        check_vma=False,
    )
```

```python
import functools
import math

import jax
import jax.numpy as jnp
from jax import lax
from jax.experimental import pallas as pl
from jax.experimental.pallas import tpu as pltpu
from jax.sharding import PartitionSpec as P

MESH = pl.DeviceIdType.MESH
EPSILON = 1e-06
LOWEST = -3e38
F32 = jnp.float32
BF16 = jnp.bfloat16

NT = (((1,), (1,)), ((), ()))
NN = (((1,), (0,)), ((), ()))


def sign_of(seeds, columns):
    mixed = seeds + columns * 747796405
    for multiplier, distance in ((1103515245, 16), (1664525, 13), (22695477, 16)):
        mixed = mixed & 2147483647
        mixed = mixed ^ jnp.right_shift(mixed, distance)
        mixed = mixed * multiplier
    mixed = mixed & 2147483647
    parity = jnp.right_shift(mixed, 17) & 1
    return (1 - 2 * parity).astype(F32)


def dot(a, b, dims):
    return lax.dot_general(a, b, dims, preferred_element_type=F32)


def split(value):
    high = value.astype(BF16)
    return high, (value - high.astype(F32)).astype(BF16)


def kernel(nz, nyh, nq, np_, scale, root_k, *refs):
    (
        (x_ref, g_ref, len_ref, red_ref, exp_ref, wseed_ref, rseed_ref, val_ref, tp_ref, inf_ref),
        (x_v, g_v, len_v, red_v, exp_v, wseed_v, rseed_v, rpad, val_v, u, r1, r2, uf, ra, rb, ha, hb, t, ts, r4, xf, xr, xs),
        (tg, tm, tx, lt, vf, vb, vq, rq, sc, r5, fp, fz),
        (in_sem, small_sem, s1, d1, s2, d2, s3, d3, s4, d4, s6, d6, s7, d7, sv, dv, sq, dq, s8, d8, s9, d9, s10, d10, near, near2, far),
    ) = refs[:10], refs[10:33], refs[33:45], refs[45:]
    nmp = 2 * nq
    el = x_v.shape[0]
    k1 = nmp * 2
    per = 2 * k1
    half_e = el // 2
    piece_e = half_e // np_
    half_rows = half_e * per
    piece_rows = piece_e * per
    chunk = piece_rows // nq
    tokens = x_v.shape[1]
    width = x_v.shape[2]
    vl = val_v.shape[0]
    te = 2 * el
    er = nyh * el // nmp
    hv = nz * vl // 2

    dp = lax.axis_index("dp")
    m = lax.axis_index("mp")
    q = lax.div(m, 2)
    c = lax.rem(m, 2)
    other = 1 - c
    z = lax.div(dp, nyh)
    yh = lax.rem(dp, nyh)
    sibling = (dp, 2 * q + other)

    nx = nq // 2
    ylo = lax.div(q, nx)
    x = lax.rem(q, nx)

    def ring_hops(d, n):
        return min(d, n - d)

    chips = [(dy, dx) for dy in range(2) for dx in range(nx) if (dy, dx) != (0, 0)]
    chips.sort(key=lambda d: -(d[0] + ring_hops(d[1], nx)))
    group = [(dy, dx, dc) for dy in range(2) for dx in range(nx) for dc in range(2) if (dy, dx, dc) != (0, 0, 0)]
    group.sort(key=lambda d: -(d[0] + ring_hops(d[1], nx)))
    depths = sorted(range(1, nz), key=lambda d: -ring_hops(d, nz))
    lines = sorted(range(1, nyh), key=lambda d: -ring_hops(d, nyh))

    def chip_at(shift, sign=1):
        return lax.rem(ylo + shift[0], 2) * nx + lax.rem(x + nx + sign * shift[1], nx)

    def member(shift):
        return 2 * chip_at(shift) + lax.rem(c + shift[2], 2)

    def chip(p):
        return (dp, 2 * p + c)

    def column(zz):
        return (zz * nyh + yh, m)

    def row(yy, mm):
        return (z * nyh + yy, mm)

    def remote(src, dst, send, recv, device):
        return pltpu.make_async_remote_copy(
            src_ref=src, dst_ref=dst, send_sem=send, recv_sem=recv, device_id=device, device_id_type=MESH
        )

    pieces = [(h, k) for h in (other, c) for k in range(np_)]

    def examples(h, k):
        return pl.ds((2 * k + h) * piece_e, piece_e)

    inputs = []
    for i, (h, k) in enumerate(pieces):
        inputs.append(
            (
                pltpu.make_async_copy(x_ref.at[examples(h, k)], x_v.at[examples(h, k)], in_sem.at[0, i]),
                pltpu.make_async_copy(g_ref.at[examples(h, k)], g_v.at[examples(h, k)], in_sem.at[1, i]),
            )
        )
    small = [
        pltpu.make_async_copy(a, b, small_sem.at[i])
        for i, (a, b) in enumerate(
            (
                (rseed_ref, rseed_v),
                (red_ref, red_v),
                (exp_ref, exp_v),
                (len_ref, len_v),
                (val_ref, val_v),
                (wseed_ref, wseed_v),
            )
        )
    ]
    for copy in small[:3] + list(inputs[0]):
        copy.start()

    barrier = pltpu.get_barrier_semaphore()

    def turns(n):
        return sorted({1 % n, (n - 1) % n} - {0})

    def along_y(s):
        y = lax.rem(2 * yh + ylo + s, 2 * nyh)
        return (z * nyh + lax.div(y, 2), 2 * (lax.rem(y, 2) * nx + x) + c)

    def signal(semaphore, device):
        pl.semaphore_signal(semaphore, inc=1, device_id=device, device_id_type=MESH)

    in_plane = [chip(chip_at((0, s))) for s in turns(nx)] + [along_y(s) for s in turns(2 * nyh)]
    planes = [column(lax.rem(z + s, nz)) for s in turns(nz)]
    sides = turns(nyh)
    for device in [sibling] + in_plane + planes:
        signal(barrier, device)
    for copy in [small[3]] + [copy for pair in inputs[1:] for copy in pair] + small[4:]:
        copy.start()

    others = [(dyh, *shift) for dyh in range(nyh) for shift in [(0, 0, 0)] + group if (dyh, *shift) != (0, 0, 0, 0)]
    others.sort(key=lambda d: -(2 * ring_hops(d[0], nyh) + d[1] + ring_hops(d[2], nx)))

    def neighbour(dyh, *shift):
        return lax.rem(yh + dyh, nyh), member(shift)

    rpad[...] = jnp.zeros_like(rpad)
    small[0].wait()
    rpad[0:2, 0:k1] = rseed_v[...]
    ranks = lax.broadcasted_iota(jnp.int32, (128, 128), 0)
    left_a = sign_of(rpad[0:1, :], ranks).T[0:k1].astype(BF16)
    left_b = sign_of(rpad[1:2, :], ranks).T[0:k1].astype(BF16)
    small[1].wait()
    small[2].wait()
    p_out = jnp.concatenate(split(dot(left_a, exp_v[...], NT)), axis=0)
    p_in = jnp.concatenate(split(dot(left_b, red_v[...], NN)), axis=0)
    small[3].wait()

    lane_t = lax.broadcasted_iota(jnp.int32, (k1, tokens), 1)

    def sketch(h, k):
        def body(i, carry):
            e = (2 * k + h) * piece_e + i
            kept = lane_t < len_v[e]
            out = dot(p_out, g_v[e], NT)
            inn = dot(p_in, x_v[e], NT)
            base = pl.multiple_of(h * half_rows + k * piece_rows + i * per, per)
            u[pl.ds(base, k1), :] = jnp.where(kept, out[:k1] + out[k1:], 0.0)
            u[pl.ds(base + k1, k1), :] = jnp.where(kept, inn[:k1] + inn[k1:], 0.0)
            return carry

        return body

    def sketch_piece(i):
        h, k = pieces[i]
        for copy in inputs[i]:
            copy.wait()
        lax.fori_loop(0, piece_e, sketch(h, k), 0, unroll=True)

    def rows_of(h, k):
        return pl.ds(pl.multiple_of(h * half_rows + k * piece_rows, piece_rows), piece_rows)

    def chunk_of(h, k, p):
        return pl.ds(pl.multiple_of(h * half_rows + k * piece_rows + p * chunk, chunk), chunk)

    def lend(k):
        return remote(u.at[rows_of(other, k)], r1.at[k], s1.at[k], d1.at[k], sibling)

    def spread(k, i):
        p = chip_at(chips[i])
        return remote(u.at[chunk_of(c, k, p)], r2.at[k, i], s2.at[k], d2.at[k], chip(p))

    def spread_all(k):
        return remote(r2.at[k], r2.at[k], s2.at[k], d2.at[k], chip(q))

    def borrowed(k, p):
        return u[chunk_of(c, k, p), :] + r1[k, pl.ds(pl.multiple_of(p * chunk, chunk), chunk), :]

    outer = [i for i, shift in enumerate(chips) if shift[0] + ring_hops(shift[1], nx) > 2]

    def spread_piece(k):
        lend(k).wait_recv()
        for i, shift in enumerate(chips):
            p = chip_at(shift)
            u[chunk_of(c, k, p), :] = borrowed(k, p)
            if k or i not in outer:
                spread(k, i).start()

    def along(i, offset, shift, part):
        at = lax.rem(z + nz + offset, nz)
        block = vf.at[at] if part is None else vf.at[at, pl.ds(part * (vl // 2), vl // 2)]
        return remote(block, block, sv.at[i], dv.at[i], column(lax.rem(z + nz + shift, nz)))

    def arrival(i, offset, shift, part):
        at = lax.rem(z + 2 * nz + offset - shift, nz)
        block = vf.at[at] if part is None else vf.at[at, pl.ds(part * (vl // 2), vl // 2)]
        return remote(block, block, sv.at[i], dv.at[i], column(lax.rem(z + nz - shift, nz)))

    first_hop = [(0, 0, 1, None), (1, 0, -1, None)]
    if nz == 8:
        second_hop = [(2, -1, 1, None), (3, 1, -1, None)]
        third_hop = [(4, -2, 1, None), (5, 2, -1, None), (6, -2, 2, 0), (7, 2, -2, 1)]
    else:
        second_hop = []
        third_hop = [(2, -1, 1, 0), (3, 1, -1, 1)]

    sketch_piece(0)
    pl.semaphore_wait(barrier, 1 + len(in_plane) + len(planes))
    lend(0).start()
    for device in in_plane:
        signal(near, device)
    small[4].wait()
    vf[z] = val_v[...].astype(F32)
    for hop in first_hop:
        along(*hop).start()
    for k in range(1, np_):
        sketch_piece(k)
        lend(k).start()
    sketch_piece(np_)
    pl.semaphore_wait(near, len(in_plane))
    signal(near2, (dp, 2 * chip_at((1, 0)) + c))
    for j in sides:
        signal(far, row(lax.rem(yh + j, nyh), m))
    spread_piece(0)
    pl.semaphore_wait(near2, 1)
    for i in outer:
        spread(0, i).start()
    for k in range(1, np_):
        sketch_piece(np_ + k)
        spread_piece(k)

    def trade(k, side):
        part = pl.ds(k * piece_e, piece_e)
        return remote(xf.at[side, part], xr.at[side, part], s4.at[k, side], d4.at[k, side], sibling)

    for k in range(np_):
        for side, tokens_v in enumerate((x_v, g_v)):

            def widen(i, carry, side=side, tokens_v=tokens_v, k=k):
                xf[side, k * piece_e + i] = tokens_v[(2 * k + other) * piece_e + i].astype(F32)
                return carry

            lax.fori_loop(0, piece_e, widen, 0)
            trade(k, side).start()

    small[5].wait()
    for s, device in enumerate((m, 2 * q + other)):
        columns = device * width + lax.broadcasted_iota(jnp.int32, (width, wseed_v.shape[1]), 0)
        ra[s] = sign_of(wseed_v[0:1, :], columns).astype(BF16)
        rb[s] = sign_of(wseed_v[1:2, :], columns).astype(BF16)
    for hop in first_hop:
        arrival(*hop).wait_recv()
    for hop in second_hop:
        along(*hop).start()

    def hand_out(k, i):
        part = uf.at[chunk_of(0, k, q)]
        return remote(part, part, s3.at[k], d3.at[k], chip(chip_at(chips[i])))

    def landed(k):
        return remote(r2.at[k], r2.at[k], s3.at[k], d3.at[k], chip(q))

    for k in range(np_):
        own = borrowed(k, q)
        spread_all(k).wait_recv()
        for j in range(1, nq):
            own = own + r2[k, j - 1]
        uf[chunk_of(0, k, q), :] = own
        for i in range(len(chips)):
            hand_out(k, i).start()

    for k in range(np_):
        for side in range(2):
            trade(k, side).wait_recv()

            def narrow_tokens(i, carry, side=side, k=k):
                xs[side, k * piece_e + i] = xr[side, k * piece_e + i].astype(BF16)
                return carry

            lax.fori_loop(0, piece_e, narrow_tokens, 0)
    for hop in second_hop[:2]:
        arrival(*hop).wait_recv()
    for hop in third_hop:
        along(*hop).start()

    def project(k, j):
        i = k * piece_e + j
        base = i * per
        a = jnp.concatenate(split(uf[pl.ds(base, k1), :]), axis=0)
        b = jnp.concatenate(split(uf[pl.ds(base + k1, k1), :]), axis=0)
        at = pl.ds(i * k1, k1)
        e = (2 * k + c) * piece_e + j
        for s, (xe, ge) in enumerate(((x_v[e], g_v[e]), (xs[0, i], xs[1, i]))):
            down_part = dot(a, xe, NN)
            up_part = dot(b, ge, NN)
            for h, part in ((ha, down_part), (hb, up_part)):
                high, low = split(part[:k1] + part[k1:])
                h[s, 0, at, :] = high
                h[s, 1, at, :] = low

    def combine(k):
        size = piece_e * k1
        at = pl.ds(k * size, size)
        total = 0.0
        for s in range(2):
            for h, r in ((ha, ra), (hb, rb)):
                total = total + dot(jnp.concatenate([h[s, 0, at, :], h[s, 1, at, :]], axis=0), r[s], NN)
        total = (total[:size] + total[size:]) * scale
        t[0, at, :] = total[:, :128]
        t[1, at, :] = total[:, 128:]

    block = 4 * piece_e

    def block_of(p):
        return pl.ds(pl.multiple_of(p * block, block), block)

    def regroup(k):
        for side in range(2):
            for al in range(2):
                for j in range(piece_e):
                    to = pl.ds((2 * side + al) * piece_e + j, nmp, stride=block)
                    ts[k, to, :] = t[side, pl.ds((k * piece_e + j) * k1 + al, nmp, stride=2), :]

    def scatter(k, i):
        p = member(group[i])
        return remote(ts.at[k, block_of(p)], r4.at[k, i], s6.at[k], d6.at[k], (dp, p))

    def scatter_all(k):
        return remote(r4.at[k], r4.at[k], s6.at[k], d6.at[k], (dp, m))

    for k in range(np_):
        landed(k).wait_recv()
        for j in range(piece_e):
            project(k, j)
        combine(k)
        regroup(k)
        for i in range(len(group)):
            scatter(k, i).start()

    each = 2 * block

    def share(k, j):
        part = tg.at[pl.ds(pl.multiple_of((yh * np_ + k) * each, each), each)]
        return remote(part, part, s7.at[k], d7.at[k], row(lax.rem(yh + j, nyh), m))

    def shared(k):
        part = tg.at[pl.ds(0, (nyh - 1) * each)]
        return remote(part, part, s7.at[k], d7.at[k], row(yh, m))

    if sides:
        pl.semaphore_wait(far, len(sides))
    for k in range(np_):
        scatter_all(k).wait_recv()
        mine, theirs = ts[k, block_of(m), :], 0.0
        for i, shift in enumerate(group):
            if shift[2]:
                theirs = theirs + r4[k, i]
            else:
                mine = mine + r4[k, i]
        pair = jnp.concatenate([jnp.where(c == 0, mine, theirs), jnp.where(c == 0, theirs, mine)], axis=0)
        tg[pl.ds(pl.multiple_of((yh * np_ + k) * each, each), each), :] = pair
        tm[k * each : (k + 1) * each, :] = pair
        for j in lines:
            share(k, j).start()

    def unfold(target, source, first, at):
        for side in range(2):
            for al in range(2):
                for j in range(piece_e):
                    rows = pl.ds(at + (2 * side + al) * piece_e + j, 2 * np_, stride=block)
                    target[2 * al + side, pl.ds(first + j, 2 * np_, stride=piece_e), :] = source[rows, :]

    unfold(tx, tm, 0, 0)
    for i in range(4):
        tp_ref[:, i * 128 : (i + 1) * 128] = tx[i]
    for hop in second_hop[2:] + third_hop:
        arrival(*hop).wait_recv()

    def narrow(i, carry):
        vb[pl.ds(pl.multiple_of(i * vl, vl), vl), :] = vf[i].astype(BF16)
        return carry

    lax.fori_loop(0, nz, narrow, 0)
    ones = jnp.ones((16, vf.shape[2]), BF16)
    wide = vb[...].astype(F32)
    high, low = split(wide * wide)
    vq[0] = (dot(ones, high, NT) + dot(ones, low, NT))[0:1]

    def tally(i):
        return remote(vq.at[0], rq.at[i], sq.at[0], dq.at[0], (dp, member(group[i])))

    tally_all = remote(rq, rq, sq.at[0], dq.at[0], (dp, m))
    for i in range(len(group)):
        tally(i).start()
    sc[...] = jnp.zeros_like(sc)

    if nyh > 1:
        for k in range(np_):
            shared(k).wait_recv()

    for y in range(nyh):
        unfold(lt, tg, y * el, y * np_ * each)
    train = jnp.concatenate([lt[i] for i in range(4)], axis=1)
    rows = nyh * el
    scores = dot(jnp.concatenate(split(train), axis=0), vb[...], NT)
    scores = scores[:rows] + scores[rows:]
    high, low = split(train * train)
    squares = (dot(ones, high, NT) + dot(ones, low, NT))[0:1]
    for i in range(nmp):
        sc[i, 0:er, :] = scores[i * er : (i + 1) * er, 0:hv]
        sc[i, er : 2 * er, :] = scores[i * er : (i + 1) * er, hv : 2 * hv]
        sc[i, 2 * er : 2 * er + 1, 0:rows] = squares

    def deal(i):
        p = member(group[i])
        return remote(sc.at[p], r5.at[i], s8.at[0], d8.at[0], (dp, p))

    deal_all = remote(r5, r5, s8.at[0], d8.at[0], (dp, m))
    for i in range(len(group)):
        deal(i).start()
    tally_all.wait_recv()
    norms = vq[0]
    for j in range(1, nmp):
        norms = norms + rq[j - 1]
    norms = lax.rsqrt(norms + EPSILON)
    row_id = lax.broadcasted_iota(jnp.int32, (8, hv), 0)
    lane_id = lax.broadcasted_iota(jnp.int32, (8, hv), 1)
    norms = jnp.where(row_id < er, norms[:, 0:hv], norms[:, hv : 2 * hv])
    deal_all.wait_recv()
    summed = sc[m]
    for j in range(1, nmp):
        summed = summed + r5[j - 1]

    cosines = summed * norms
    e_of = jnp.where(row_id < er, row_id, row_id - er)
    squares = jnp.sum(
        jnp.where(lane_id == m * er + e_of, summed[2 * er : 2 * er + 1, :], 0.0), axis=1, keepdims=True
    )
    weight = lax.rsqrt(squares + EPSILON) * root_k
    row_o = lax.broadcasted_iota(jnp.int32, (8, 128), 0)
    lane_o = lax.broadcasted_iota(jnp.int32, (8, 128), 1)
    placed = jnp.full((8, 128), LOWEST, F32)
    start = lax.rem(m, 4) * (er * nz)
    first_half = row_o < er
    e_of = jnp.where(first_half, row_o, row_o - er)
    for g in range(nz // 2):
        here = (lane_id >= g * vl) & (lane_id < (g + 1) * vl)
        best = jnp.max(jnp.where(here, cosines, LOWEST), axis=1, keepdims=True) * weight
        lane = start + e_of * nz + jnp.where(first_half, 0, nz // 2) + g
        placed = jnp.where((lane_o == lane) & (row_o < 2 * er), best, placed)
    place = yh * nmp + m
    fp[place] = jnp.max(placed, axis=0, keepdims=True)

    def tell(shift):
        part = fp.at[place]
        return remote(part, part, s9.at[0], d9.at[0], row(*neighbour(*shift)))

    told = remote(fp.at[pl.ds(0, len(others))], fp.at[pl.ds(0, len(others))], s9.at[0], d9.at[0], row(yh, m))
    for shift in others:
        tell(shift).start()
    told.wait_recv()
    best = [fp[4 * i : 4 * i + 4] for i in range(nyh * nmp // 4)]
    for i in range(nmp // 4):
        fz[z, i] = jnp.max(functools.reduce(jnp.maximum, best[i :: nmp // 4]), axis=0)

    def publish(j):
        part = fz.at[z]
        return remote(part, part, s10.at[0], d10.at[0], column(lax.rem(z + j, nz)))

    published = remote(fz.at[pl.ds(0, nz - 1)], fz.at[pl.ds(0, nz - 1)], s10.at[0], d10.at[0], column(z))
    for j in depths:
        publish(j).start()

    for k in range(np_):
        lend(k).wait_send()
        spread_all(k).wait_send()
        landed(k).wait_send()
        for side in range(2):
            trade(k, side).wait_send()
    for k in range(np_):
        scatter_all(k).wait_send()
    for hop in first_hop + second_hop + third_hop:
        along(*hop).wait_send()
    tally_all.wait_send()
    if nyh > 1:
        for k in range(np_):
            shared(k).wait_send()
    deal_all.wait_send()
    told.wait_send()
    published.wait_recv()
    inf_ref[...] = fz[...]
    published.wait_send()


def on_device(nz, nyh, nq, np_, scale, root_k, *args):
    inputs, _, lengths, reducing, expanding, wseeds, rseeds, validation = args
    el, tokens, width = inputs.shape
    nmp = 2 * nq
    k1 = 2 * nmp
    vl, kl = validation.shape
    k2 = wseeds.shape[1]
    half_rows = el * k1
    piece_rows = half_rows // np_
    chunk = piece_rows // nq
    hv = nz * vl // 2
    dma = pltpu.SemaphoreType.DMA
    scratch = [
        pltpu.VMEM(inputs.shape, BF16),
        pltpu.VMEM(inputs.shape, BF16),
        pltpu.SMEM(lengths.shape, jnp.int32),
        pltpu.VMEM(reducing.shape, BF16),
        pltpu.VMEM(expanding.shape, BF16),
        pltpu.VMEM(wseeds.shape, jnp.int32),
        pltpu.VMEM(rseeds.shape, jnp.int32),
        pltpu.VMEM((8, 128), jnp.int32),
        pltpu.VMEM(validation.shape, BF16),
        pltpu.VMEM((2 * half_rows, tokens), F32),
        pltpu.VMEM((np_, piece_rows, tokens), F32),
        pltpu.VMEM((np_, nq - 1, chunk, tokens), F32),
        pltpu.VMEM((half_rows, tokens), F32),
        pltpu.VMEM((2, width, k2), BF16),
        pltpu.VMEM((2, width, k2), BF16),
        pltpu.VMEM((2, 2, el * k1 // 2, width), BF16),
        pltpu.VMEM((2, 2, el * k1 // 2, width), BF16),
        pltpu.VMEM((2, el * k1 // 2, 128), F32),
        pltpu.VMEM((np_, nmp * 2 * el // np_, 128), F32),
        pltpu.VMEM((np_, nmp - 1, 2 * el // np_, 128), F32),
        pltpu.VMEM((2, el // 2, tokens, width), F32),
        pltpu.VMEM((2, el // 2, tokens, width), F32),
        pltpu.VMEM((2, el // 2, tokens, width), BF16),
        pltpu.VMEM((nyh * 4 * el, 128), F32),
        pltpu.VMEM((4 * el, 128), F32),
        pltpu.VMEM((4, el, 128), F32),
        pltpu.VMEM((4, nyh * el, 128), F32),
        pltpu.VMEM((nz, vl, kl), F32),
        pltpu.VMEM((nz * vl, kl), BF16),
        pltpu.VMEM((1, 1, nz * vl), F32),
        pltpu.VMEM((nmp - 1, 1, nz * vl), F32),
        pltpu.VMEM((nmp, 8, hv), F32),
        pltpu.VMEM((nmp - 1, 8, hv), F32),
        pltpu.VMEM((nyh * nmp, 1, 128), F32),
        pltpu.VMEM((nz, nmp // 4, 1, 128), F32),
        dma((2, 2 * np_)),
        dma((6,)),
    ]
    one = (1,)
    for count in (
        (np_,),
        (np_,),
        (np_,),
        (np_, 2),
        (np_,),
        (np_,),
        (nz,),
        one,
        one,
        one,
        one,
    ):
        scratch += [dma(count), dma(count)]
    scratch += [pltpu.SemaphoreType.REGULAR] * 3
    train_proj, best = pl.pallas_call(
        functools.partial(kernel, nz, nyh, nq, np_, scale, root_k),
        out_shape=(
            jax.ShapeDtypeStruct((el, kl), F32),
            jax.ShapeDtypeStruct((nz, nmp // 4, 1, 128), F32),
        ),
        in_specs=[pl.BlockSpec(memory_space=pltpu.HBM)] * len(args),
        out_specs=[pl.BlockSpec(memory_space=pltpu.VMEM)] * 2,
        scratch_shapes=scratch,
        compiler_params=pltpu.CompilerParams(
            collective_id=0, has_side_effects=True, vmem_limit_bytes=48 * 1024 * 1024
        ),
    )(*[pltpu.with_memory_space_constraint(a, pltpu.HBM) for a in args])
    er = nyh * el // nmp
    influence = best.reshape(nz * nmp // 4, 128)[:, : 4 * er * nz].reshape(nz * nmp * er, nz)
    return (train_proj, influence)


def solution(mesh, nyh=4, np_=3):
    ndp, nmp = mesh.shape["dp"], mesh.shape["mp"]
    nz, nq = ndp // nyh, nmp // 2
    width = nmp * 256
    scale = 1.0 / math.sqrt(2.0 * 128 * width * 256)
    root_k = math.sqrt(2 * nmp * 256)
    in_specs = (
        P("dp", None, "mp"),
        P("dp", None, "mp"),
        P("dp"),
        P(None, "mp"),
        P("mp", None),
        P(),
        P(),
        P("dp", "mp"),
    )
    return jax.shard_map(
        functools.partial(on_device, nz, nyh, nq, np_, scale, root_k),
        mesh=mesh,
        in_specs=in_specs,
        out_specs=(P("dp", "mp"), P()),
        check_vma=False,
    )
```

```python
import functools
import math

import jax
import jax.numpy as jnp
from jax import lax
from jax.experimental import pallas as pl
from jax.experimental.pallas import tpu as pltpu
from jax.sharding import PartitionSpec as P

MESH = pl.DeviceIdType.MESH
EPSILON = 1e-06
LOWEST = -3e38
F32 = jnp.float32
BF16 = jnp.bfloat16

NT = (((1,), (1,)), ((), ()))
NN = (((1,), (0,)), ((), ()))


def sign_of(seeds, columns):
    mixed = seeds + columns * 747796405
    for multiplier, distance in ((1103515245, 16), (1664525, 13), (22695477, 16)):
        mixed = mixed & 2147483647
        mixed = mixed ^ jnp.right_shift(mixed, distance)
        mixed = mixed * multiplier
    mixed = mixed & 2147483647
    parity = jnp.right_shift(mixed, 17) & 1
    return (1 - 2 * parity).astype(F32)


def dot(a, b, dims):
    return lax.dot_general(a, b, dims, preferred_element_type=F32)


def split(value):
    high = value.astype(BF16)
    return high, (value - high.astype(F32)).astype(BF16)


def kernel(nz, nyh, nq, np_, scale, root_k, *refs):
    (
        (x_ref, g_ref, len_ref, red_ref, exp_ref, wseed_ref, rseed_ref, val_ref, tp_ref, inf_ref),
        (x_v, g_v, len_v, red_v, exp_v, wseed_v, rseed_v, rpad, val_v, u, r1, r2, uf, ra, rb, ha, hb, t, ts, r4, xf, xr, xs),
        (tg, tm, tx, lt, vf, vb, vq, rq, sc, r5, fp, fz),
        (in_sem, small_sem, s1, d1, s2, d2, s3, d3, s4, d4, s6, d6, s7, d7, sv, dv, sq, dq, s8, d8, s9, d9, s10, d10, near, near2, far),
    ) = refs[:10], refs[10:33], refs[33:45], refs[45:]
    nmp = 2 * nq
    el = x_v.shape[0]
    k1 = nmp * 2
    per = 2 * k1
    half_e = el // 2
    piece_e = half_e // np_
    half_rows = half_e * per
    piece_rows = piece_e * per
    chunk = piece_rows // nq
    tokens = x_v.shape[1]
    width = x_v.shape[2]
    vl = val_v.shape[0]
    te = 2 * el
    er = nyh * el // nmp
    hv = nz * vl // 2

    dp = lax.axis_index("dp")
    m = lax.axis_index("mp")
    q = lax.div(m, 2)
    c = lax.rem(m, 2)
    other = 1 - c
    z = lax.div(dp, nyh)
    yh = lax.rem(dp, nyh)
    sibling = (dp, 2 * q + other)

    nx = nq // 2
    ylo = lax.div(q, nx)
    x = lax.rem(q, nx)

    def ring_hops(d, n):
        return min(d, n - d)

    chips = [(dy, dx) for dy in range(2) for dx in range(nx) if (dy, dx) != (0, 0)]
    chips.sort(key=lambda d: -(d[0] + ring_hops(d[1], nx)))
    group = [(dy, dx, dc) for dy in range(2) for dx in range(nx) for dc in range(2) if (dy, dx, dc) != (0, 0, 0)]
    group.sort(key=lambda d: -(d[0] + ring_hops(d[1], nx)))
    depths = sorted(range(1, nz), key=lambda d: -ring_hops(d, nz))
    lines = sorted(range(1, nyh), key=lambda d: -ring_hops(d, nyh))

    def chip_at(shift, sign=1):
        return lax.rem(ylo + shift[0], 2) * nx + lax.rem(x + nx + sign * shift[1], nx)

    def member(shift):
        return 2 * chip_at(shift) + lax.rem(c + shift[2], 2)

    def chip(p):
        return (dp, 2 * p + c)

    def column(zz):
        return (zz * nyh + yh, m)

    def row(yy, mm):
        return (z * nyh + yy, mm)

    def remote(src, dst, send, recv, device):
        return pltpu.make_async_remote_copy(
            src_ref=src, dst_ref=dst, send_sem=send, recv_sem=recv, device_id=device, device_id_type=MESH
        )

    pieces = [(h, k) for h in (other, c) for k in range(np_)]

    def examples(k):
        return pl.ds(2 * k * piece_e, 2 * piece_e)

    inputs = [
        [
            pltpu.make_async_copy(a.at[examples(k)], b.at[examples(k)], in_sem.at[k])
            for a, b in ((x_ref, x_v), (g_ref, g_v))
        ]
        for k in range(np_)
    ]

    def inputs_in(k):
        both = pl.ds(0, 4 * piece_e)
        pltpu.make_async_copy(x_ref.at[both], x_v.at[both], in_sem.at[k]).wait()

    small = [
        pltpu.make_async_copy(a, b, small_sem.at[i])
        for i, a, b in (
            (0, rseed_ref, rseed_v),
            (1, red_ref, red_v),
            (1, exp_ref, exp_v),
            (2, len_ref, len_v),
            (3, val_ref, val_v),
            (4, wseed_ref, wseed_v),
        )
    ]
    for copy in small[:4] + inputs[0]:
        copy.start()

    barrier = pltpu.get_barrier_semaphore()

    def turns(n):
        return sorted({1 % n, (n - 1) % n} - {0})

    def along_y(s):
        y = lax.rem(2 * yh + ylo + s, 2 * nyh)
        return (z * nyh + lax.div(y, 2), 2 * (lax.rem(y, 2) * nx + x) + c)

    def signal(semaphore, device):
        pl.semaphore_signal(semaphore, inc=1, device_id=device, device_id_type=MESH)

    in_plane = [chip(chip_at((0, s))) for s in turns(nx)] + [along_y(s) for s in turns(2 * nyh)]
    planes = [column(lax.rem(z + s, nz)) for s in turns(nz)]
    sides = turns(nyh)
    for device in [sibling] + in_plane + planes:
        signal(barrier, device)
    for copy in small[4:5] + [copy for pair in inputs[1:] for copy in pair] + small[5:]:
        copy.start()

    others = [(dyh, *shift) for dyh in range(nyh) for shift in [(0, 0, 0)] + group if (dyh, *shift) != (0, 0, 0, 0)]
    others.sort(key=lambda d: -(2 * ring_hops(d[0], nyh) + d[1] + ring_hops(d[2], nx)))

    def neighbour(dyh, *shift):
        return lax.rem(yh + dyh, nyh), member(shift)

    rpad[...] = jnp.zeros_like(rpad)
    small[0].wait()
    rpad[0:2, 0:k1] = rseed_v[...]
    ranks = lax.broadcasted_iota(jnp.int32, (128, 128), 0)
    left_a = sign_of(rpad[0:1, :], ranks).T[0:k1].astype(BF16)
    left_b = sign_of(rpad[1:2, :], ranks).T[0:k1].astype(BF16)
    pltpu.make_async_copy(x_ref.at[0], x_v.at[0], small_sem.at[1]).wait()
    p_out = jnp.concatenate(split(dot(left_a, exp_v[...], NT)), axis=0)
    p_in = jnp.concatenate(split(dot(left_b, red_v[...], NN)), axis=0)
    small[3].wait()

    lane_t = lax.broadcasted_iota(jnp.int32, (k1, tokens), 1)

    def sketch(h, k):
        def body(i, carry):
            e = (2 * k + h) * piece_e + i
            kept = lane_t < len_v[e]
            out = dot(p_out, g_v[e], NT)
            inn = dot(p_in, x_v[e], NT)
            base = pl.multiple_of(h * half_rows + k * piece_rows + i * per, per)
            u[pl.ds(base, k1), :] = jnp.where(kept, out[:k1] + out[k1:], 0.0)
            u[pl.ds(base + k1, k1), :] = jnp.where(kept, inn[:k1] + inn[k1:], 0.0)
            return carry

        return body

    def sketch_piece(i):
        h, k = pieces[i]
        if i < np_:
            inputs_in(k)
        lax.fori_loop(0, piece_e, sketch(h, k), 0, unroll=True)

    def rows_of(h, k):
        return pl.ds(pl.multiple_of(h * half_rows + k * piece_rows, piece_rows), piece_rows)

    def chunk_of(h, k, p):
        return pl.ds(pl.multiple_of(h * half_rows + k * piece_rows + p * chunk, chunk), chunk)

    def lend(k):
        return remote(u.at[rows_of(other, k)], r1.at[k], s1.at[0], d1.at[k], sibling)

    def spread(k, i):
        p = chip_at(chips[i])
        return remote(u.at[chunk_of(c, k, p)], r2.at[k, i], s2.at[0], d2.at[k], chip(p))

    def spread_all(k):
        return remote(r2.at[k], r2.at[k], s2.at[0], d2.at[k], chip(q))

    def borrowed(k, p):
        return u[chunk_of(c, k, p), :] + r1[k, pl.ds(pl.multiple_of(p * chunk, chunk), chunk), :]

    outer = [i for i, shift in enumerate(chips) if shift[0] + ring_hops(shift[1], nx) > 2]

    def spread_piece(k):
        lend(k).wait_recv()
        for i, shift in enumerate(chips):
            p = chip_at(shift)
            u[chunk_of(c, k, p), :] = borrowed(k, p)
            if k or i not in outer:
                spread(k, i).start()

    def along(i, offset, shift, part):
        at = lax.rem(z + nz + offset, nz)
        block = vf.at[at] if part is None else vf.at[at, pl.ds(part * (vl // 2), vl // 2)]
        return remote(block, block, sv.at[0], dv.at[i], column(lax.rem(z + nz + shift, nz)))

    def arrived(i, blocks):
        block = vf.at[pl.ds(0, blocks)]
        return remote(block, block, sv.at[0], dv.at[i], column(z))

    first_hop = [(0, 0, 1, None), (0, 0, -1, None)]
    if nz == 8:
        second_hop = [(1, -1, 1, None), (1, 1, -1, None)]
        third_hop = [(2, -2, 1, None), (2, 2, -1, None), (2, -2, 2, 0), (2, 2, -2, 1)]
    else:
        second_hop = []
        third_hop = [(2, -1, 1, 0), (2, 1, -1, 1)]

    sketch_piece(0)
    pl.semaphore_wait(barrier, 1 + len(in_plane) + len(planes))
    lend(0).start()
    for device in in_plane:
        signal(near, device)
    small[4].wait()
    vf[z] = val_v[...].astype(F32)
    for hop in first_hop:
        along(*hop).start()
    for k in range(1, np_):
        sketch_piece(k)
        lend(k).start()
    sketch_piece(np_)
    pl.semaphore_wait(near, len(in_plane))
    signal(near2, (dp, 2 * chip_at((1, 0)) + c))
    for j in sides:
        signal(far, row(lax.rem(yh + j, nyh), m))
    spread_piece(0)
    ahead = min(1, np_ - 1)
    for k in range(1, ahead + 1):
        sketch_piece(np_ + k)
    pl.semaphore_wait(near2, 1)
    for i in outer:
        spread(0, i).start()
    for k in range(1, np_):
        if k > ahead:
            sketch_piece(np_ + k)
        spread_piece(k)

    def trade(k, side):
        part = pl.ds(k * piece_e, piece_e)
        return remote(xf.at[side, part], xr.at[side, part], s4.at[0], d4.at[k], sibling)

    for k in range(np_):
        for side, tokens_v in enumerate((x_v, g_v)):

            def widen(i, carry, side=side, tokens_v=tokens_v, k=k):
                xf[side, k * piece_e + i] = tokens_v[(2 * k + other) * piece_e + i].astype(F32)
                return carry

            lax.fori_loop(0, piece_e, widen, 0)
            trade(k, side).start()

    small[5].wait()
    for s, device in enumerate((m, 2 * q + other)):
        columns = device * width + lax.broadcasted_iota(jnp.int32, (width, wseed_v.shape[1]), 0)
        ra[s] = sign_of(wseed_v[0:1, :], columns).astype(BF16)
        rb[s] = sign_of(wseed_v[1:2, :], columns).astype(BF16)
    arrived(0, 2).wait_recv()
    for hop in second_hop:
        along(*hop).start()

    def hand_out(k, i):
        part = uf.at[chunk_of(0, k, q)]
        return remote(part, part, s3.at[0], d3.at[k], chip(chip_at(chips[i])))

    def landed(k):
        return remote(r2.at[k], r2.at[k], s3.at[0], d3.at[k], chip(q))

    for k in range(np_):
        own = borrowed(k, q)
        spread_all(k).wait_recv()
        for j in range(1, nq):
            own = own + r2[k, j - 1]
        uf[chunk_of(0, k, q), :] = own
        for i in range(len(chips)):
            hand_out(k, i).start()

    for k in range(np_):
        traded = xr.at[0, pl.ds(0, 2 * piece_e)]
        remote(traded, traded, s4.at[0], d4.at[k], sibling).wait_recv()
        for side in range(2):

            def narrow_tokens(i, carry, side=side, k=k):
                xs[side, k * piece_e + i] = xr[side, k * piece_e + i].astype(BF16)
                return carry

            lax.fori_loop(0, piece_e, narrow_tokens, 0)
    if second_hop:
        arrived(1, 2).wait_recv()
    for hop in third_hop:
        along(*hop).start()

    def project(k, j):
        i = k * piece_e + j
        base = i * per
        a = jnp.concatenate(split(uf[pl.ds(base, k1), :]), axis=0)
        b = jnp.concatenate(split(uf[pl.ds(base + k1, k1), :]), axis=0)
        at = pl.ds(i * k1, k1)
        e = (2 * k + c) * piece_e + j
        for s, (xe, ge) in enumerate(((x_v[e], g_v[e]), (xs[0, i], xs[1, i]))):
            down_part = dot(a, xe, NN)
            up_part = dot(b, ge, NN)
            for h, part in ((ha, down_part), (hb, up_part)):
                high, low = split(part[:k1] + part[k1:])
                h[s, 0, at, :] = high
                h[s, 1, at, :] = low

    def combine(k):
        size = piece_e * k1
        at = pl.ds(k * size, size)
        total = 0.0
        for s in range(2):
            for h, r in ((ha, ra), (hb, rb)):
                total = total + dot(jnp.concatenate([h[s, 0, at, :], h[s, 1, at, :]], axis=0), r[s], NN)
        total = (total[:size] + total[size:]) * scale
        t[0, at, :] = total[:, :128]
        t[1, at, :] = total[:, 128:]

    block = 4 * piece_e

    def block_of(p):
        return pl.ds(pl.multiple_of(p * block, block), block)

    def regroup(k):
        for side in range(2):
            for al in range(2):
                for j in range(piece_e):
                    to = pl.ds((2 * side + al) * piece_e + j, nmp, stride=block)
                    ts[k, to, :] = t[side, pl.ds((k * piece_e + j) * k1 + al, nmp, stride=2), :]

    def scatter(k, i):
        p = member(group[i])
        return remote(ts.at[k, block_of(p)], r4.at[k, i], s6.at[0], d6.at[k], (dp, p))

    def scatter_all(k):
        return remote(r4.at[k], r4.at[k], s6.at[0], d6.at[k], (dp, m))

    for k in range(np_):
        landed(k).wait_recv()
        for j in range(piece_e):
            project(k, j)
        combine(k)
        regroup(k)
        for i in range(len(group)):
            scatter(k, i).start()

    each = 2 * block

    def share(k, j):
        part = tg.at[pl.ds(pl.multiple_of((yh * np_ + k) * each, each), each)]
        return remote(part, part, s7.at[0], d7.at[k], row(lax.rem(yh + j, nyh), m))

    def shared(k):
        part = tg.at[pl.ds(0, (nyh - 1) * each)]
        return remote(part, part, s7.at[0], d7.at[k], row(yh, m))

    if sides:
        pl.semaphore_wait(far, len(sides))
    for k in range(np_):
        scatter_all(k).wait_recv()
        mine, theirs = ts[k, block_of(m), :], 0.0
        for i, shift in enumerate(group):
            if shift[2]:
                theirs = theirs + r4[k, i]
            else:
                mine = mine + r4[k, i]
        pair = jnp.concatenate([jnp.where(c == 0, mine, theirs), jnp.where(c == 0, theirs, mine)], axis=0)
        tg[pl.ds(pl.multiple_of((yh * np_ + k) * each, each), each), :] = pair
        tm[k * each : (k + 1) * each, :] = pair
        for j in lines:
            share(k, j).start()

    def unfold(target, source, first, at):
        for side in range(2):
            for al in range(2):
                for j in range(piece_e):
                    rows = pl.ds(at + (2 * side + al) * piece_e + j, 2 * np_, stride=block)
                    target[2 * al + side, pl.ds(first + j, 2 * np_, stride=piece_e), :] = source[rows, :]

    unfold(tx, tm, 0, 0)
    for i in range(4):
        tp_ref[:, i * 128 : (i + 1) * 128] = tx[i]
    arrived(2, nz - 5 if second_hop else nz - 3).wait_recv()

    def narrow(i, carry):
        vb[pl.ds(pl.multiple_of(i * vl, vl), vl), :] = vf[i].astype(BF16)
        return carry

    lax.fori_loop(0, nz, narrow, 0)
    ones = jnp.ones((16, vf.shape[2]), BF16)
    wide = vb[...].astype(F32)
    high, low = split(wide * wide)
    vq[0] = (dot(ones, high, NT) + dot(ones, low, NT))[0:1]

    def tally(i):
        return remote(vq.at[0], rq.at[i], sq.at[0], dq.at[0], (dp, member(group[i])))

    tally_all = remote(rq, rq, sq.at[0], dq.at[0], (dp, m))
    for i in range(len(group)):
        tally(i).start()
    sc[...] = jnp.zeros_like(sc)

    if nyh > 1:
        for k in range(np_):
            shared(k).wait_recv()

    for y in range(nyh):
        unfold(lt, tg, y * el, y * np_ * each)
    train = jnp.concatenate([lt[i] for i in range(4)], axis=1)
    rows = nyh * el
    scores = dot(jnp.concatenate(split(train), axis=0), vb[...], NT)
    scores = scores[:rows] + scores[rows:]
    high, low = split(train * train)
    squares = (dot(ones, high, NT) + dot(ones, low, NT))[0:1]
    for i in range(nmp):
        sc[i, 0:er, :] = scores[i * er : (i + 1) * er, 0:hv]
        sc[i, er : 2 * er, :] = scores[i * er : (i + 1) * er, hv : 2 * hv]
        sc[i, 2 * er : 2 * er + 1, 0:rows] = squares

    def deal(i):
        p = member(group[i])
        return remote(sc.at[p], r5.at[i], s8.at[0], d8.at[0], (dp, p))

    deal_all = remote(r5, r5, s8.at[0], d8.at[0], (dp, m))
    for i in range(len(group)):
        deal(i).start()
    tally_all.wait_recv()
    norms = vq[0]
    for j in range(1, nmp):
        norms = norms + rq[j - 1]
    norms = lax.rsqrt(norms + EPSILON)
    row_id = lax.broadcasted_iota(jnp.int32, (8, hv), 0)
    lane_id = lax.broadcasted_iota(jnp.int32, (8, hv), 1)
    norms = jnp.where(row_id < er, norms[:, 0:hv], norms[:, hv : 2 * hv])
    deal_all.wait_recv()
    summed = sc[m]
    for j in range(1, nmp):
        summed = summed + r5[j - 1]

    cosines = summed * norms
    e_of = jnp.where(row_id < er, row_id, row_id - er)
    squares = jnp.sum(
        jnp.where(lane_id == m * er + e_of, summed[2 * er : 2 * er + 1, :], 0.0), axis=1, keepdims=True
    )
    weight = lax.rsqrt(squares + EPSILON) * root_k
    row_o = lax.broadcasted_iota(jnp.int32, (8, 128), 0)
    lane_o = lax.broadcasted_iota(jnp.int32, (8, 128), 1)
    placed = jnp.full((8, 128), LOWEST, F32)
    start = lax.rem(m, 4) * (er * nz)
    first_half = row_o < er
    e_of = jnp.where(first_half, row_o, row_o - er)
    for g in range(nz // 2):
        here = (lane_id >= g * vl) & (lane_id < (g + 1) * vl)
        best = jnp.max(jnp.where(here, cosines, LOWEST), axis=1, keepdims=True) * weight
        lane = start + e_of * nz + jnp.where(first_half, 0, nz // 2) + g
        placed = jnp.where((lane_o == lane) & (row_o < 2 * er), best, placed)
    place = yh * nmp + m
    fp[place] = jnp.max(placed, axis=0, keepdims=True)

    def tell(shift):
        part = fp.at[place]
        return remote(part, part, s9.at[0], d9.at[0], row(*neighbour(*shift)))

    told = remote(fp.at[pl.ds(0, len(others))], fp.at[pl.ds(0, len(others))], s9.at[0], d9.at[0], row(yh, m))
    for shift in others:
        tell(shift).start()
    told.wait_recv()
    best = [fp[4 * i : 4 * i + 4] for i in range(nyh * nmp // 4)]
    for i in range(nmp // 4):
        fz[z, i] = jnp.max(functools.reduce(jnp.maximum, best[i :: nmp // 4]), axis=0)

    def publish(j):
        part = fz.at[z]
        return remote(part, part, s10.at[0], d10.at[0], column(lax.rem(z + j, nz)))

    published = remote(fz.at[pl.ds(0, nz - 1)], fz.at[pl.ds(0, nz - 1)], s10.at[0], d10.at[0], column(z))
    for j in depths:
        publish(j).start()

    remote(r1, r1, s1.at[0], d1.at[0], sibling).wait_send()
    remote(r2, r2, s2.at[0], d2.at[0], sibling).wait_send()
    remote(r2, r2, s3.at[0], d3.at[0], sibling).wait_send()
    remote(xr, xr, s4.at[0], d4.at[0], sibling).wait_send()
    remote(r4, r4, s6.at[0], d6.at[0], sibling).wait_send()
    arrived(0, nz - 1).wait_send()
    tally_all.wait_send()
    if nyh > 1:
        sent = tg.at[pl.ds(0, (nyh - 1) * np_ * each)]
        remote(sent, sent, s7.at[0], d7.at[0], sibling).wait_send()
    deal_all.wait_send()
    told.wait_send()
    published.wait_recv()
    inf_ref[...] = fz[...]
    published.wait_send()


def on_device(nz, nyh, nq, np_, scale, root_k, *args):
    inputs, _, lengths, reducing, expanding, wseeds, rseeds, validation = args
    el, tokens, width = inputs.shape
    nmp = 2 * nq
    k1 = 2 * nmp
    vl, kl = validation.shape
    k2 = wseeds.shape[1]
    half_rows = el * k1
    piece_rows = half_rows // np_
    chunk = piece_rows // nq
    hv = nz * vl // 2
    dma = pltpu.SemaphoreType.DMA
    scratch = [
        pltpu.VMEM(inputs.shape, BF16),
        pltpu.VMEM(inputs.shape, BF16),
        pltpu.SMEM(lengths.shape, jnp.int32),
        pltpu.VMEM(reducing.shape, BF16),
        pltpu.VMEM(expanding.shape, BF16),
        pltpu.VMEM(wseeds.shape, jnp.int32),
        pltpu.VMEM(rseeds.shape, jnp.int32),
        pltpu.VMEM((8, 128), jnp.int32),
        pltpu.VMEM(validation.shape, BF16),
        pltpu.VMEM((2 * half_rows, tokens), F32),
        pltpu.VMEM((np_, piece_rows, tokens), F32),
        pltpu.VMEM((np_, nq - 1, chunk, tokens), F32),
        pltpu.VMEM((half_rows, tokens), F32),
        pltpu.VMEM((2, width, k2), BF16),
        pltpu.VMEM((2, width, k2), BF16),
        pltpu.VMEM((2, 2, el * k1 // 2, width), BF16),
        pltpu.VMEM((2, 2, el * k1 // 2, width), BF16),
        pltpu.VMEM((2, el * k1 // 2, 128), F32),
        pltpu.VMEM((np_, nmp * 2 * el // np_, 128), F32),
        pltpu.VMEM((np_, nmp - 1, 2 * el // np_, 128), F32),
        pltpu.VMEM((2, el // 2, tokens, width), F32),
        pltpu.VMEM((2, el // 2, tokens, width), F32),
        pltpu.VMEM((2, el // 2, tokens, width), BF16),
        pltpu.VMEM((nyh * 4 * el, 128), F32),
        pltpu.VMEM((4 * el, 128), F32),
        pltpu.VMEM((4, el, 128), F32),
        pltpu.VMEM((4, nyh * el, 128), F32),
        pltpu.VMEM((nz, vl, kl), F32),
        pltpu.VMEM((nz * vl, kl), BF16),
        pltpu.VMEM((1, 1, nz * vl), F32),
        pltpu.VMEM((nmp - 1, 1, nz * vl), F32),
        pltpu.VMEM((nmp, 8, hv), F32),
        pltpu.VMEM((nmp - 1, 8, hv), F32),
        pltpu.VMEM((nyh * nmp, 1, 128), F32),
        pltpu.VMEM((nz, nmp // 4, 1, 128), F32),
        dma((np_,)),
        dma((5,)),
    ]
    for receives in (np_,) * 6 + (3,) + (1,) * 4:
        scratch += [dma((1,)), dma((receives,))]
    scratch += [pltpu.SemaphoreType.REGULAR] * 3
    train_proj, best = pl.pallas_call(
        functools.partial(kernel, nz, nyh, nq, np_, scale, root_k),
        out_shape=(
            jax.ShapeDtypeStruct((el, kl), F32),
            jax.ShapeDtypeStruct((nz, nmp // 4, 1, 128), F32),
        ),
        in_specs=[pl.BlockSpec(memory_space=pltpu.HBM)] * len(args),
        out_specs=[pl.BlockSpec(memory_space=pltpu.VMEM)] * 2,
        scratch_shapes=scratch,
        compiler_params=pltpu.CompilerParams(
            collective_id=0, has_side_effects=True, vmem_limit_bytes=48 * 1024 * 1024
        ),
    )(*[pltpu.with_memory_space_constraint(a, pltpu.HBM) for a in args])
    er = nyh * el // nmp
    influence = best.reshape(nz * nmp // 4, 128)[:, : 4 * er * nz].reshape(nz * nmp * er, nz)
    return (train_proj, influence)


def solution(mesh, nyh=4, np_=3):
    ndp, nmp = mesh.shape["dp"], mesh.shape["mp"]
    nz, nq = ndp // nyh, nmp // 2
    width = nmp * 256
    scale = 1.0 / math.sqrt(2.0 * 128 * width * 256)
    root_k = math.sqrt(2 * nmp * 256)
    in_specs = (
        P("dp", None, "mp"),
        P("dp", None, "mp"),
        P("dp"),
        P(None, "mp"),
        P("mp", None),
        P(),
        P(),
        P("dp", "mp"),
    )
    return jax.shard_map(
        functools.partial(on_device, nz, nyh, nq, np_, scale, root_k),
        mesh=mesh,
        in_specs=in_specs,
        out_specs=(P("dp", "mp"), P()),
        check_vma=False,
    )
```

```python
import functools
import math

import jax
import jax.numpy as jnp
from jax import lax
from jax.experimental import pallas as pl
from jax.experimental.pallas import tpu as pltpu
from jax.sharding import PartitionSpec as P

MESH = pl.DeviceIdType.MESH
EPSILON = 1e-06
LOWEST = -3e38
F32 = jnp.float32
BF16 = jnp.bfloat16

NT = (((1,), (1,)), ((), ()))
NN = (((1,), (0,)), ((), ()))


def sign_of(seeds, columns):
    mixed = seeds + columns * 747796405
    for multiplier, distance in ((1103515245, 16), (1664525, 13), (22695477, 16)):
        mixed = mixed & 2147483647
        mixed = mixed ^ jnp.right_shift(mixed, distance)
        mixed = mixed * multiplier
    mixed = mixed & 2147483647
    parity = jnp.right_shift(mixed, 17) & 1
    return (1 - 2 * parity).astype(F32)


def dot(a, b, dims):
    return lax.dot_general(a, b, dims, preferred_element_type=F32)


def split(value):
    high = value.astype(BF16)
    return high, (value - high.astype(F32)).astype(BF16)


def kernel(nz, nyh, nq, np_, scale, root_k, *refs):
    (
        (x_ref, g_ref, len_ref, red_ref, exp_ref, wseed_ref, rseed_ref, val_ref, tp_ref, inf_ref),
        (x_v, g_v, len_v, red_v, exp_v, wseed_v, rseed_v, rpad, val_v, u, r1, r2, uf, ra, rb, ha, hb, t, ts, r4, xf, xr, xs),
        (tg, tm, tx, lt, vf, vb, vq, rq, sc, r5, fp, fz),
        (in_sem, small_sem, s1, d1, s2, d2, s3, d3, s4, d4, s6, d6, s7, d7, sv, dv, sq, dq, s8, d8, s9, d9, s10, d10, near, near2, far),
    ) = refs[:10], refs[10:33], refs[33:45], refs[45:]
    nmp = 2 * nq
    el = x_v.shape[0]
    k1 = nmp * 2
    per = 2 * k1
    half_e = el // 2
    piece_e = half_e // np_
    half_rows = half_e * per
    piece_rows = piece_e * per
    chunk = piece_rows // nq
    tokens = x_v.shape[1]
    width = x_v.shape[2]
    vl = val_v.shape[0]
    te = 2 * el
    er = nyh * el // nmp
    hv = nz * vl // 2

    dp = lax.axis_index("dp")
    m = lax.axis_index("mp")
    q = lax.div(m, 2)
    c = lax.rem(m, 2)
    other = 1 - c
    z = lax.div(dp, nyh)
    yh = lax.rem(dp, nyh)
    sibling = (dp, 2 * q + other)

    nx = nq // 2
    ylo = lax.div(q, nx)
    x = lax.rem(q, nx)

    def ring_hops(d, n):
        return min(d, n - d)

    chips = [(dy, dx) for dy in range(2) for dx in range(nx) if (dy, dx) != (0, 0)]
    chips.sort(key=lambda d: -(d[0] + ring_hops(d[1], nx)))
    group = [(dy, dx, dc) for dy in range(2) for dx in range(nx) for dc in range(2) if (dy, dx, dc) != (0, 0, 0)]
    group.sort(key=lambda d: -(d[0] + ring_hops(d[1], nx)))
    depths = sorted(range(1, nz), key=lambda d: -ring_hops(d, nz))
    lines = sorted(range(1, nyh), key=lambda d: -ring_hops(d, nyh))

    def chip_at(shift, sign=1):
        return lax.rem(ylo + shift[0], 2) * nx + lax.rem(x + nx + sign * shift[1], nx)

    def member(shift):
        return 2 * chip_at(shift) + lax.rem(c + shift[2], 2)

    def chip(p):
        return (dp, 2 * p + c)

    def column(zz):
        return (zz * nyh + yh, m)

    def row(yy, mm):
        return (z * nyh + yy, mm)

    def remote(src, dst, send, recv, device):
        return pltpu.make_async_remote_copy(
            src_ref=src, dst_ref=dst, send_sem=send, recv_sem=recv, device_id=device, device_id_type=MESH
        )

    pieces = [(h, k) for h in (other, c) for k in range(np_)]

    def examples(k):
        return pl.ds(2 * k * piece_e, 2 * piece_e)

    inputs = [
        [
            pltpu.make_async_copy(a.at[examples(k)], b.at[examples(k)], in_sem.at[k])
            for a, b in ((x_ref, x_v), (g_ref, g_v))
        ]
        for k in range(np_)
    ]

    def inputs_in(k):
        both = pl.ds(0, 4 * piece_e)
        pltpu.make_async_copy(x_ref.at[both], x_v.at[both], in_sem.at[k]).wait()

    small = [
        pltpu.make_async_copy(a, b, small_sem.at[i])
        for i, a, b in (
            (0, rseed_ref, rseed_v),
            (1, red_ref, red_v),
            (1, exp_ref, exp_v),
            (2, len_ref, len_v),
            (3, val_ref, val_v),
            (4, wseed_ref, wseed_v),
        )
    ]
    for copy in small[:4] + inputs[0]:
        copy.start()

    barrier = pltpu.get_barrier_semaphore()

    def turns(n):
        return sorted({1 % n, (n - 1) % n} - {0})

    def along_y(s):
        y = lax.rem(2 * yh + ylo + s, 2 * nyh)
        return (z * nyh + lax.div(y, 2), 2 * (lax.rem(y, 2) * nx + x) + c)

    def signal(semaphore, device):
        pl.semaphore_signal(semaphore, inc=1, device_id=device, device_id_type=MESH)

    in_plane = [chip(chip_at((0, s))) for s in turns(nx)] + [along_y(s) for s in turns(2 * nyh)]
    planes = [column(lax.rem(z + s, nz)) for s in turns(nz)]
    sides = turns(nyh)
    for device in [sibling] + in_plane + planes:
        signal(barrier, device)
    for copy in small[4:5] + [copy for pair in inputs[1:] for copy in pair] + small[5:]:
        copy.start()

    others = [(dyh, *shift) for dyh in range(nyh) for shift in [(0, 0, 0)] + group if (dyh, *shift) != (0, 0, 0, 0)]
    others.sort(key=lambda d: -(2 * ring_hops(d[0], nyh) + d[1] + ring_hops(d[2], nx)))

    def neighbour(dyh, *shift):
        return lax.rem(yh + dyh, nyh), member(shift)

    rpad[...] = jnp.zeros_like(rpad)
    small[0].wait()
    rpad[0:2, 0:k1] = rseed_v[...]
    ranks = lax.broadcasted_iota(jnp.int32, (128, 128), 0)
    left_a = sign_of(rpad[0:1, :], ranks).T[0:k1].astype(BF16)
    left_b = sign_of(rpad[1:2, :], ranks).T[0:k1].astype(BF16)
    pltpu.make_async_copy(x_ref.at[0], x_v.at[0], small_sem.at[1]).wait()
    p_out = jnp.concatenate(split(dot(left_a, exp_v[...], NT)), axis=0)
    p_in = jnp.concatenate(split(dot(left_b, red_v[...], NN)), axis=0)
    small[3].wait()

    lane_t = lax.broadcasted_iota(jnp.int32, (k1, tokens), 1)

    def sketch(h, k):
        def body(i, carry):
            e = (2 * k + h) * piece_e + i
            kept = lane_t < len_v[e]
            out = dot(p_out, g_v[e], NT)
            inn = dot(p_in, x_v[e], NT)
            base = pl.multiple_of(h * half_rows + k * piece_rows + i * per, per)
            u[pl.ds(base, k1), :] = jnp.where(kept, out[:k1] + out[k1:], 0.0)
            u[pl.ds(base + k1, k1), :] = jnp.where(kept, inn[:k1] + inn[k1:], 0.0)
            return carry

        return body

    def sketch_piece(i):
        h, k = pieces[i]
        if i < np_:
            inputs_in(k)
        lax.fori_loop(0, piece_e, sketch(h, k), 0, unroll=True)

    def rows_of(h, k):
        return pl.ds(pl.multiple_of(h * half_rows + k * piece_rows, piece_rows), piece_rows)

    def chunk_of(h, k, p):
        return pl.ds(pl.multiple_of(h * half_rows + k * piece_rows + p * chunk, chunk), chunk)

    def lend(k):
        return remote(u.at[rows_of(other, k)], r1.at[k], s1.at[0], d1.at[k], sibling)

    def spread(k, i):
        p = chip_at(chips[i])
        return remote(u.at[chunk_of(c, k, p)], r2.at[k, i], s2.at[0], d2.at[k], chip(p))

    def spread_all(k):
        return remote(r2.at[k], r2.at[k], s2.at[0], d2.at[k], chip(q))

    def borrowed(k, p):
        return u[chunk_of(c, k, p), :] + r1[k, pl.ds(pl.multiple_of(p * chunk, chunk), chunk), :]

    outer = [i for i, shift in enumerate(chips) if shift[0] + ring_hops(shift[1], nx) > 2]

    def spread_piece(k):
        lend(k).wait_recv()
        for i, shift in enumerate(chips):
            p = chip_at(shift)
            u[chunk_of(c, k, p), :] = borrowed(k, p)
            if k or i not in outer:
                spread(k, i).start()

    def along(i, offset, shift, part):
        at = lax.rem(z + nz + offset, nz)
        block = vf.at[at] if part is None else vf.at[at, pl.ds(part * (vl // 2), vl // 2)]
        return remote(block, block, sv.at[0], dv.at[i], column(lax.rem(z + nz + shift, nz)))

    def arrived(i, blocks):
        block = vf.at[pl.ds(0, blocks)]
        return remote(block, block, sv.at[0], dv.at[i], column(z))

    first_hop = [(0, 0, 1, None), (0, 0, -1, None)]
    if nz == 8:
        second_hop = [(1, -1, 1, None), (1, 1, -1, None)]
        third_hop = [(2, -2, 1, None), (2, 2, -1, None), (2, -2, 2, 0), (2, 2, -2, 1)]
    else:
        second_hop = []
        third_hop = [(2, -1, 1, 0), (2, 1, -1, 1)]

    sketch_piece(0)
    pl.semaphore_wait(barrier, 1 + len(in_plane) + len(planes))
    lend(0).start()
    for device in in_plane:
        signal(near, device)
    small[4].wait()
    vf[z] = val_v[...].astype(F32)
    for hop in first_hop:
        along(*hop).start()
    for k in range(1, np_):
        sketch_piece(k)
        lend(k).start()
    sketch_piece(np_)
    pl.semaphore_wait(near, len(in_plane))
    signal(near2, (dp, 2 * chip_at((1, 0)) + c))
    for j in sides:
        signal(far, row(lax.rem(yh + j, nyh), m))
    spread_piece(0)
    ahead = min(1, np_ - 1)
    for k in range(1, ahead + 1):
        sketch_piece(np_ + k)
    pl.semaphore_wait(near2, 1)
    for i in outer:
        spread(0, i).start()
    for k in range(1, np_):
        if k > ahead:
            sketch_piece(np_ + k)
        spread_piece(k)

    def trade(k, side):
        part = pl.ds(k * piece_e, piece_e)
        return remote(xf.at[side, part], xr.at[side, part], s4.at[0], d4.at[k], sibling)

    for k in range(np_):
        for side, tokens_v in enumerate((x_v, g_v)):

            def widen(i, carry, side=side, tokens_v=tokens_v, k=k):
                xf[side, k * piece_e + i] = tokens_v[(2 * k + other) * piece_e + i].astype(F32)
                return carry

            lax.fori_loop(0, piece_e, widen, 0)
            trade(k, side).start()

    small[5].wait()
    for s, device in enumerate((m, 2 * q + other)):
        columns = device * width + lax.broadcasted_iota(jnp.int32, (width, wseed_v.shape[1]), 0)
        ra[s] = sign_of(wseed_v[0:1, :], columns).astype(BF16)
        rb[s] = sign_of(wseed_v[1:2, :], columns).astype(BF16)
    arrived(0, 2).wait_recv()
    for hop in second_hop:
        along(*hop).start()

    def hand_out(k, i):
        part = uf.at[chunk_of(0, k, q)]
        return remote(part, part, s3.at[0], d3.at[k], chip(chip_at(chips[i])))

    def landed(k):
        return remote(r2.at[k], r2.at[k], s3.at[0], d3.at[k], chip(q))

    for k in range(np_):
        own = borrowed(k, q)
        spread_all(k).wait_recv()
        for j in range(1, nq):
            own = own + r2[k, j - 1]
        uf[chunk_of(0, k, q), :] = own
        for i in range(len(chips)):
            hand_out(k, i).start()

    for k in range(np_):
        traded = xr.at[0, pl.ds(0, 2 * piece_e)]
        remote(traded, traded, s4.at[0], d4.at[k], sibling).wait_recv()
        for side in range(2):

            def narrow_tokens(i, carry, side=side, k=k):
                xs[side, k * piece_e + i] = xr[side, k * piece_e + i].astype(BF16)
                return carry

            lax.fori_loop(0, piece_e, narrow_tokens, 0)
    if second_hop:
        arrived(1, 2).wait_recv()
    for hop in third_hop:
        along(*hop).start()

    def project(k, j):
        i = k * piece_e + j
        base = i * per
        a = jnp.concatenate(split(uf[pl.ds(base, k1), :]), axis=0)
        b = jnp.concatenate(split(uf[pl.ds(base + k1, k1), :]), axis=0)
        at = pl.ds(i * k1, k1)
        e = (2 * k + c) * piece_e + j
        for s, (xe, ge) in enumerate(((x_v[e], g_v[e]), (xs[0, i], xs[1, i]))):
            down_part = dot(a, xe, NN)
            up_part = dot(b, ge, NN)
            for h, part in ((ha, down_part), (hb, up_part)):
                high, low = split(part[:k1] + part[k1:])
                h[s, 0, at, :] = high
                h[s, 1, at, :] = low

    def combine(k):
        size = piece_e * k1
        at = pl.ds(k * size, size)
        total = 0.0
        for s in range(2):
            for h, r in ((ha, ra), (hb, rb)):
                total = total + dot(jnp.concatenate([h[s, 0, at, :], h[s, 1, at, :]], axis=0), r[s], NN)
        total = (total[:size] + total[size:]) * scale
        t[0, at, :] = total[:, :128]
        t[1, at, :] = total[:, 128:]

    block = 4 * piece_e

    def block_of(p):
        return pl.ds(pl.multiple_of(p * block, block), block)

    def regroup(k):
        for side in range(2):
            for al in range(2):
                for j in range(piece_e):
                    to = pl.ds((2 * side + al) * piece_e + j, nmp, stride=block)
                    ts[k, to, :] = t[side, pl.ds((k * piece_e + j) * k1 + al, nmp, stride=2), :]

    def scatter(k, i):
        p = member(group[i])
        return remote(ts.at[k, block_of(p)], r4.at[k, i], s6.at[0], d6.at[k], (dp, p))

    def scatter_all(k):
        return remote(r4.at[k], r4.at[k], s6.at[0], d6.at[k], (dp, m))

    for k in range(np_):
        landed(k).wait_recv()
        for j in range(piece_e):
            project(k, j)
        combine(k)
        regroup(k)
        for i in range(len(group)):
            scatter(k, i).start()

    each = 2 * block

    def share(k, j):
        part = tg.at[pl.ds(pl.multiple_of((yh * np_ + k) * each, each), each)]
        return remote(part, part, s7.at[0], d7.at[k], row(lax.rem(yh + j, nyh), m))

    def shared(k):
        part = tg.at[pl.ds(0, (nyh - 1) * each)]
        return remote(part, part, s7.at[0], d7.at[k], row(yh, m))

    if sides:
        pl.semaphore_wait(far, len(sides))
    for k in range(np_):
        scatter_all(k).wait_recv()
        mine, theirs = ts[k, block_of(m), :], 0.0
        for i, shift in enumerate(group):
            if shift[2]:
                theirs = theirs + r4[k, i]
            else:
                mine = mine + r4[k, i]
        pair = jnp.concatenate([jnp.where(c == 0, mine, theirs), jnp.where(c == 0, theirs, mine)], axis=0)
        tg[pl.ds(pl.multiple_of((yh * np_ + k) * each, each), each), :] = pair
        tm[k * each : (k + 1) * each, :] = pair
        for j in lines:
            share(k, j).start()

    def unfold(target, source, first, at):
        for side in range(2):
            for al in range(2):
                for j in range(piece_e):
                    rows = pl.ds(at + (2 * side + al) * piece_e + j, 2 * np_, stride=block)
                    target[2 * al + side, pl.ds(first + j, 2 * np_, stride=piece_e), :] = source[rows, :]

    unfold(tx, tm, 0, 0)
    for i in range(4):
        tp_ref[:, i * 128 : (i + 1) * 128] = tx[i, 0:el, :]
    arrived(2, nz - 5 if second_hop else nz - 3).wait_recv()

    def narrow(i, carry):
        vb[pl.ds(pl.multiple_of(i * vl, vl), vl), :] = vf[i].astype(BF16)
        return carry

    lax.fori_loop(0, nz, narrow, 0)
    ones = jnp.ones((16, vf.shape[2]), BF16)
    wide = vb[...].astype(F32)
    high, low = split(wide * wide)
    vq[0] = (dot(ones, high, NT) + dot(ones, low, NT))[0:1]

    def tally(i):
        return remote(vq.at[0], rq.at[i], sq.at[0], dq.at[0], (dp, member(group[i])))

    tally_all = remote(rq, rq, sq.at[0], dq.at[0], (dp, m))
    for i in range(len(group)):
        tally(i).start()
    sc[...] = jnp.zeros_like(sc)

    if nyh > 1:
        for k in range(np_):
            shared(k).wait_recv()

    for y in range(nyh):
        unfold(lt, tg, y * el, y * np_ * each)
    train = jnp.concatenate([lt[i, 0 : nyh * el, :] for i in range(4)], axis=1)
    rows = nyh * el
    scores = dot(jnp.concatenate(split(train), axis=0), vb[...], NT)
    scores = scores[:rows] + scores[rows:]
    high, low = split(train * train)
    squares = (dot(ones, high, NT) + dot(ones, low, NT))[0:1]
    for i in range(nmp):
        sc[i, 0:er, :] = scores[i * er : (i + 1) * er, 0:hv]
        sc[i, er : 2 * er, :] = scores[i * er : (i + 1) * er, hv : 2 * hv]
        sc[i, 2 * er : 2 * er + 1, 0:rows] = squares

    def deal(i):
        p = member(group[i])
        return remote(sc.at[p], r5.at[i], s8.at[0], d8.at[0], (dp, p))

    deal_all = remote(r5, r5, s8.at[0], d8.at[0], (dp, m))
    for i in range(len(group)):
        deal(i).start()
    tally_all.wait_recv()
    norms = vq[0]
    for j in range(1, nmp):
        norms = norms + rq[j - 1]
    norms = lax.rsqrt(norms + EPSILON)
    row_id = lax.broadcasted_iota(jnp.int32, (8, hv), 0)
    lane_id = lax.broadcasted_iota(jnp.int32, (8, hv), 1)
    norms = jnp.where(row_id < er, norms[:, 0:hv], norms[:, hv : 2 * hv])
    deal_all.wait_recv()
    summed = sc[m]
    for j in range(1, nmp):
        summed = summed + r5[j - 1]

    cosines = summed * norms
    e_of = jnp.where(row_id < er, row_id, row_id - er)
    squares = jnp.sum(
        jnp.where(lane_id == m * er + e_of, summed[2 * er : 2 * er + 1, :], 0.0), axis=1, keepdims=True
    )
    weight = lax.rsqrt(squares + EPSILON) * root_k
    row_o = lax.broadcasted_iota(jnp.int32, (8, 128), 0)
    lane_o = lax.broadcasted_iota(jnp.int32, (8, 128), 1)
    placed = jnp.full((8, 128), LOWEST, F32)
    start = lax.rem(m, 4) * (er * nz)
    first_half = row_o < er
    e_of = jnp.where(first_half, row_o, row_o - er)
    for g in range(nz // 2):
        here = (lane_id >= g * vl) & (lane_id < (g + 1) * vl)
        best = jnp.max(jnp.where(here, cosines, LOWEST), axis=1, keepdims=True) * weight
        lane = start + e_of * nz + jnp.where(first_half, 0, nz // 2) + g
        placed = jnp.where((lane_o == lane) & (row_o < 2 * er), best, placed)
    place = yh * nmp + m
    fp[place] = jnp.max(placed, axis=0, keepdims=True)

    def tell(shift):
        part = fp.at[place]
        return remote(part, part, s9.at[0], d9.at[0], row(*neighbour(*shift)))

    told = remote(fp.at[pl.ds(0, len(others))], fp.at[pl.ds(0, len(others))], s9.at[0], d9.at[0], row(yh, m))
    for shift in others:
        tell(shift).start()
    told.wait_recv()
    best = [fp[4 * i : 4 * i + 4] for i in range(nyh * nmp // 4)]
    for i in range(nmp // 4):
        fz[z, i] = jnp.max(functools.reduce(jnp.maximum, best[i :: nmp // 4]), axis=0)

    def publish(j):
        part = fz.at[z]
        return remote(part, part, s10.at[0], d10.at[0], column(lax.rem(z + j, nz)))

    published = remote(fz.at[pl.ds(0, nz - 1)], fz.at[pl.ds(0, nz - 1)], s10.at[0], d10.at[0], column(z))
    for j in depths:
        publish(j).start()

    remote(r1, r1, s1.at[0], d1.at[0], sibling).wait_send()
    remote(r2, r2, s2.at[0], d2.at[0], sibling).wait_send()
    remote(r2, r2, s3.at[0], d3.at[0], sibling).wait_send()
    remote(xr, xr, s4.at[0], d4.at[0], sibling).wait_send()
    remote(r4, r4, s6.at[0], d6.at[0], sibling).wait_send()
    arrived(0, nz - 1).wait_send()
    tally_all.wait_send()
    if nyh > 1:
        sent = tg.at[pl.ds(0, (nyh - 1) * np_ * each)]
        remote(sent, sent, s7.at[0], d7.at[0], sibling).wait_send()
    deal_all.wait_send()
    told.wait_send()
    published.wait_recv()
    inf_ref[...] = fz[...]
    published.wait_send()


def on_device(nz, nyh, nq, np_, scale, root_k, *args):
    inputs, _, lengths, reducing, expanding, wseeds, rseeds, validation = args
    el, tokens, width = inputs.shape
    nmp = 2 * nq
    k1 = 2 * nmp
    vl, kl = validation.shape
    k2 = wseeds.shape[1]
    half_rows = el * k1
    piece_rows = half_rows // np_
    chunk = piece_rows // nq
    hv = nz * vl // 2
    dma = pltpu.SemaphoreType.DMA
    scratch = [
        pltpu.VMEM(inputs.shape, BF16),
        pltpu.VMEM(inputs.shape, BF16),
        pltpu.SMEM(lengths.shape, jnp.int32),
        pltpu.VMEM(reducing.shape, BF16),
        pltpu.VMEM(expanding.shape, BF16),
        pltpu.VMEM(wseeds.shape, jnp.int32),
        pltpu.VMEM(rseeds.shape, jnp.int32),
        pltpu.VMEM((8, 128), jnp.int32),
        pltpu.VMEM(validation.shape, BF16),
        pltpu.VMEM((2 * half_rows, tokens), F32),
        pltpu.VMEM((np_, piece_rows, tokens), F32),
        pltpu.VMEM((np_, nq - 1, chunk, tokens), F32),
        pltpu.VMEM((half_rows, tokens), F32),
        pltpu.VMEM((2, width, k2), BF16),
        pltpu.VMEM((2, width, k2), BF16),
        pltpu.VMEM((2, 2, el * k1 // 2, width), BF16),
        pltpu.VMEM((2, 2, el * k1 // 2, width), BF16),
        pltpu.VMEM((2, el * k1 // 2, 128), F32),
        pltpu.VMEM((np_, nmp * 2 * el // np_, 128), F32),
        pltpu.VMEM((np_, nmp - 1, 2 * el // np_, 128), F32),
        pltpu.VMEM((2, el // 2, tokens, width), F32),
        pltpu.VMEM((2, el // 2, tokens, width), F32),
        pltpu.VMEM((2, el // 2, tokens, width), BF16),
        pltpu.VMEM(((nyh + 1) * 4 * el, 128), F32),
        pltpu.VMEM((8 * el, 128), F32),
        pltpu.VMEM((4, 2 * el, 128), F32),
        pltpu.VMEM((4, (nyh + 2) * el, 128), F32),
        pltpu.VMEM((nz, vl, kl), F32),
        pltpu.VMEM((nz * vl, kl), BF16),
        pltpu.VMEM((1, 1, nz * vl), F32),
        pltpu.VMEM((nmp - 1, 1, nz * vl), F32),
        pltpu.VMEM((nmp + 1, 8, hv), F32),
        pltpu.VMEM((nmp - 1, 8, hv), F32),
        pltpu.VMEM((nyh * nmp, 1, 128), F32),
        pltpu.VMEM((nz, nmp // 4, 1, 128), F32),
        dma((np_,)),
        dma((5,)),
    ]
    for receives in (np_,) * 6 + (3,) + (1,) * 4:
        scratch += [dma((1,)), dma((receives,))]
    scratch += [pltpu.SemaphoreType.REGULAR] * 3
    train_proj, best = pl.pallas_call(
        functools.partial(kernel, nz, nyh, nq, np_, scale, root_k),
        out_shape=(
            jax.ShapeDtypeStruct((el, kl), F32),
            jax.ShapeDtypeStruct((nz, nmp // 4, 1, 128), F32),
        ),
        in_specs=[pl.BlockSpec(memory_space=pltpu.HBM)] * len(args),
        out_specs=[pl.BlockSpec(memory_space=pltpu.VMEM)] * 2,
        scratch_shapes=scratch,
        compiler_params=pltpu.CompilerParams(
            collective_id=0, has_side_effects=True, vmem_limit_bytes=48 * 1024 * 1024
        ),
    )(*[pltpu.with_memory_space_constraint(a, pltpu.HBM) for a in args])
    er = nyh * el // nmp
    influence = best.reshape(nz * nmp // 4, 128)[:, : 4 * er * nz].reshape(nz * nmp * er, nz)
    return (train_proj, influence)


def solution(mesh, nyh=4, np_=3):
    ndp, nmp = mesh.shape["dp"], mesh.shape["mp"]
    nz, nq = ndp // nyh, nmp // 2
    width = nmp * 256
    scale = 1.0 / math.sqrt(2.0 * 128 * width * 256)
    root_k = math.sqrt(2 * nmp * 256)
    in_specs = (
        P("dp", None, "mp"),
        P("dp", None, "mp"),
        P("dp"),
        P(None, "mp"),
        P("mp", None),
        P(),
        P(),
        P("dp", "mp"),
    )
    return jax.shard_map(
        functools.partial(on_device, nz, nyh, nq, np_, scale, root_k),
        mesh=mesh,
        in_specs=in_specs,
        out_specs=(P("dp", "mp"), P()),
        check_vma=False,
    )
```
